256 devices in a mesh: seq: 32 (over y, z), head: 8 (over x, core).
Axes of the slice: x: 4, y: 4, z: 8, core: 2. Of those that a mesh axis runs over, the one named last changes fastest.
Arguments:
- query_states: bfloat16 [1, 24576, 3072], P(None, 'seq', 'head'), may hold values from -8 to 8
- key_states: bfloat16 [1, 24576, 3072], P(None, 'seq', 'head'), may hold values from -8 to 8
- value_states: bfloat16 [1, 24576, 3072], P(None, 'seq', 'head'), may hold values from -6 to 6
- spatial_mask: int32 [16, 12, 12], replicated, may hold values from 0 to 1, as said below
- temporal_mask: int32 [12, 16, 16], replicated, may hold values from 0 to 1, as said below
- temporal_heads: int32 [8], P('head'), may hold values from 0 to 23, as said below
- out_weight: bfloat16 [3072, 3072], P('head', 'seq'), may hold values from -0.109375 to 0.109375
Outputs:
- projected: bfloat16 [1, 24576, 3072], P(None, 'seq', 'head')
The draws below stay inside these ranges and needn't reach their ends.
Inputs may be any that keep to these rules, and one draw needn't show every extreme that they name: `temporal_heads`: entries i * 1 to (i + 1) - 1 are distinct heads among i * 3 to (i + 1) * 3 - 1. `spatial_mask`: diagonal blocks are 1. `temporal_mask`: entries whose two frames are at most one apart are 1.
All inputs are finite; a program needn't handle non-finite values.
Results may differ from the reference program's by a relative error of at most 0.0057.
Values may be sent and summed in bfloat16 or wider, within the bound.
No kernel may reach another device: no remote copies, remote signals or barrier semaphores. Data moves between devices by JAX's collectives and lax.ppermute only.
A program may use at most 64 MiB of HBM per device.

```python
import math
import jax
import jax.numpy as jnp
from jax import lax

D = 3072
HEADS = 24
HD = 128
TEMPORAL = 8
BLOCK = 128
FRAME = 1536
BATCH = 1
FRAMES = 16
TOKENS = 24576
NB = 12
HEAD_DEV = 3
TEMP_DEV = 1


def draw_query_states(key, part):
    key = jax.random.fold_in(key, 1)
    shape = (BATCH, TOKENS, HEADS * HD)
    states = jnp.clip(jax.random.normal(key, shape, jnp.float32), -6.0, 6.0)
    return states.astype(jnp.bfloat16)


def draw_key_states(key, part):
    key = jax.random.fold_in(key, 2)
    shape = (BATCH, TOKENS, HEADS * HD)
    states = jnp.clip(jax.random.normal(key, shape, jnp.float32), -6.0, 6.0)
    return states.astype(jnp.bfloat16)


def draw_spatial_mask(key, part):
    key = jax.random.fold_in(key, 3)
    density = jax.random.randint(jax.random.fold_in(key, 0), (FRAMES, 1, 1), 1, 9)
    coins = jax.random.randint(jax.random.fold_in(key, 1), (FRAMES, NB, NB), 0, 8)
    diagonal = jnp.eye(NB, dtype=bool)
    return jnp.where(jnp.logical_or(coins < density, diagonal[None]), 1, 0).astype(jnp.int32)


def draw_temporal_mask(key, part):
    key = jax.random.fold_in(key, 4)
    density = jax.random.randint(jax.random.fold_in(key, 0), (NB, 1, 1), 1, 9)
    coins = jax.random.randint(jax.random.fold_in(key, 1), (NB, FRAMES, FRAMES), 0, 8)
    frame_ids = jnp.arange(FRAMES, dtype=jnp.int32)
    nearby = jnp.abs(frame_ids[:, None] - frame_ids[None, :]) <= 1
    return jnp.where(jnp.logical_or(coins < density, nearby[None]), 1, 0).astype(jnp.int32)


def draw_temporal_heads(key, part):
    key = jax.random.fold_in(key, 5)
    groups = HEADS // HEAD_DEV
    group_keys = jax.random.split(key, groups)
    orders = jax.vmap(lambda sub_key: jax.random.permutation(sub_key, HEAD_DEV))(group_keys)
    chosen = orders[:, :TEMP_DEV].astype(jnp.int32) + (jnp.arange(groups, dtype=jnp.int32) * HEAD_DEV)[:, None]
    return chosen.reshape(-1).astype(jnp.int32)


def level_of(own_key, dims, shards, least, high):
    def one(dim, blocks):
        steps = jax.random.uniform(jax.random.fold_in(jax.random.fold_in(own_key, 6), dim), (blocks,), jnp.float32, least / len(shards), high / len(shards))
        return jnp.repeat(jnp.exp(steps), dims[dim] // blocks).reshape((-1,) + (1,) * (len(dims) - dim - 1))

    loudness = one(*shards[0])
    for cut in shards[1:]:
        loudness = loudness * one(*cut)
    return loudness


def noise(own_key, extent, scale, bound, pieces=(), kind=jnp.bfloat16):
    values = jax.random.normal(own_key, extent, jnp.float32) * scale
    if len(pieces) > 0:
        values = level_of(own_key, extent, pieces, -0.22, 0.18) * values
    return jnp.clip(values, min=-bound, max=bound).astype(kind)


def setup_inputs(seed: int = 0) -> dict:
    streams_of = jax.random.split(jax.random.key(seed), 8)
    query_states = draw_query_states(jax.random.fold_in(streams_of[7], 71), 0)
    key_states = draw_key_states(jax.random.fold_in(streams_of[7], 71), 0)
    value_states = noise(streams_of[2], (BATCH, TOKENS, HEADS * HD), 1.0, 6.0, ((1, 32), (2, 8)))
    spatial_mask = draw_spatial_mask(jax.random.fold_in(streams_of[7], 71), 0)
    temporal_mask = draw_temporal_mask(jax.random.fold_in(streams_of[7], 71), 0)
    temporal_heads = draw_temporal_heads(jax.random.fold_in(streams_of[7], 71), 0)
    out_weight = noise(streams_of[6], (HEADS * HD, D), (HEADS * HD) ** -0.5, 0.109375, ((0, 8), (1, 32)))
    return dict(query_states=query_states, key_states=key_states, value_states=value_states, spatial_mask=spatial_mask, temporal_mask=temporal_mask, temporal_heads=temporal_heads, out_weight=out_weight)


def normalize(scores):
    row_max = lax.optimization_barrier(jnp.max(scores, axis=-1, keepdims=True))
    lifted = jnp.exp(scores - row_max)
    return (lifted / lax.optimization_barrier(jnp.sum(lifted, axis=-1, keepdims=True))).astype(jnp.bfloat16)

def frame_attention(queries, key_rows, value_rows, allowed):
    score_scale = 1.0 / math.sqrt(HD)
    scores = jnp.dot(queries, key_rows.T, preferred_element_type=jnp.float32) * score_scale
    scores = jnp.where(allowed, scores, -jnp.inf)
    probabilities = normalize(scores)
    return jnp.dot(probabilities, value_rows, preferred_element_type=jnp.float32).astype(jnp.bfloat16)

def head_columns(states, head_id):
    start = (head_id * HD).astype(jnp.int32)
    picked = lax.dynamic_slice_in_dim(states, start, HD, 2)
    return picked.reshape(BATCH, FRAMES, FRAME, HD)

def reference(query_states, key_states, value_states, spatial_mask, temporal_mask, temporal_heads, out_weight):
    head_ids = jnp.arange(HEADS, dtype=jnp.int32)
    is_temporal = jnp.any(temporal_heads[:, None] == head_ids[None, :], axis=0).astype(jnp.int32)
    spatial_ids = jnp.argsort(is_temporal, stable=True)[:HEADS - TEMPORAL].astype(jnp.int32)

    def spatial_head(head_id):
        q_frames = head_columns(query_states, head_id).transpose(1, 0, 2, 3)
        k_frames = head_columns(key_states, head_id).transpose(1, 0, 2, 3)
        v_frames = head_columns(value_states, head_id).transpose(1, 0, 2, 3)

        def one_frame(members):
            q_one, k_one, v_one, mask_one = members
            allowed = jnp.repeat(jnp.repeat(mask_one > 0, BLOCK, axis=0), BLOCK, axis=1)
            return jax.vmap(lambda q_clip, k_clip, v_clip: frame_attention(q_clip, k_clip, v_clip, allowed))(q_one, k_one, v_one)
        return lax.map(one_frame, (q_frames, k_frames, v_frames, spatial_mask))

    def temporal_head(head_id):
        q_all = head_columns(query_states, head_id).astype(jnp.float32)
        k_all = head_columns(key_states, head_id).astype(jnp.float32)
        v_all = head_columns(value_states, head_id)
        score_scale = 1.0 / math.sqrt(HD)
        scores = jnp.einsum('bfpd,bgpd->bpfg', q_all, k_all) * score_scale
        allowed = temporal_mask[jnp.arange(FRAME, dtype=jnp.int32) // BLOCK] > 0
        scores = jnp.where(allowed[None], scores, -jnp.inf)
        probabilities = normalize(scores)
        result = jnp.einsum('bpfg,bgpd->bfpd', probabilities.astype(jnp.float32), v_all.astype(jnp.float32))
        return result.astype(jnp.bfloat16)
    spatial_out = lax.map(spatial_head, spatial_ids)
    temporal_out = lax.map(temporal_head, temporal_heads)
    attended = jnp.zeros((BATCH, FRAMES, FRAME, HEADS, HD), jnp.bfloat16)
    attended = attended.at[:, :, :, spatial_ids].set(spatial_out.transpose(2, 1, 3, 0, 4))
    attended = attended.at[:, :, :, temporal_heads].set(temporal_out.transpose(1, 2, 3, 0, 4))
    attended = attended.reshape(BATCH * TOKENS, HEADS * HD)
    projected = jnp.dot(attended, out_weight, preferred_element_type=jnp.float32).astype(jnp.bfloat16)
    return projected.reshape(BATCH, TOKENS, D)
```

```python
import functools
import math

import jax
import jax.numpy as jnp
import numpy as np
from jax import lax
from jax.experimental import pallas as pl
from jax.experimental.pallas import tpu as pltpu
from jax.sharding import PartitionSpec as P

HD = 128
BLOCK = 128
VMEM = 56 * 1024 * 1024
BF16 = jnp.bfloat16
F32 = jnp.float32
LOG2E = math.log2(math.e)
SCALE2 = LOG2E / math.sqrt(HD)
NT = (((1,), (1,)), ((), ()))


def dot_nt(a, b):
    return lax.dot_general(a, b, NT, preferred_element_type=F32)


def dot_nn(a, b):
    return jnp.dot(a, b, preferred_element_type=F32)


def params():
    return pltpu.CompilerParams(vmem_limit_bytes=VMEM)


def cost(flops, moved):
    return pl.CostEstimate(flops=flops, bytes_accessed=moved, transcendentals=0)


def pick_columns(order, sources, rows):
    arrays = [a for a, _ in sources]
    total = arrays[0].shape[0]
    count = len(sources)

    def body(order_ref, *refs):
        out = refs[-1]
        for n in range(count):
            out[:, n * HD : (n + 1) * HD] = refs[n][...]

    return pl.pallas_call(
        body,
        out_shape=jax.ShapeDtypeStruct((total, count * HD), BF16),
        grid_spec=pltpu.PrefetchScalarGridSpec(
            num_scalar_prefetch=1,
            grid=(total // rows,),
            in_specs=[
                pl.BlockSpec((rows, HD), functools.partial(lambda i, o, slot: (i, o[slot]), slot=slot))
                for _, slot in sources
            ],
            out_specs=pl.BlockSpec((rows, count * HD), lambda i, o: (i, 0)),
        ),
        compiler_params=params(),
        cost_estimate=cost(0, 4 * total * count * HD),
    )(order, *arrays)


def weight_blocks(order, weight):
    rows, cols = weight.shape

    def body(order_ref, w_ref, out_ref):
        for n in range(rows // HD):
            piece = w_ref[pl.ds(pl.multiple_of(order_ref[n] * HD, HD), HD), :]
            out_ref[:, n * HD : (n + 1) * HD] = piece.astype(F32).T.astype(BF16)

    return pl.pallas_call(
        body,
        out_shape=jax.ShapeDtypeStruct((cols, rows), BF16),
        in_specs=[pl.BlockSpec(memory_space=pltpu.SMEM), pl.BlockSpec(memory_space=pltpu.VMEM)],
        out_specs=pl.BlockSpec(memory_space=pltpu.VMEM),
        compiler_params=params(),
    )(order, weight)


def own_half(order, q, k, v, bias):
    rows = q.shape[0]
    tile = 256
    per = tile // BLOCK

    def body(order_ref, q_ref, k_ref, v_ref, bias_ref, o_ref, m_ref, l_ref):
        keys = k_ref[...]
        values = v_ref[...]
        for n in range(per):
            part = slice(n * BLOCK, (n + 1) * BLOCK)
            s = dot_nt(q_ref[part, :], keys) * SCALE2 + bias_ref[n]
            m = jnp.max(s, axis=1, keepdims=True)
            p = jnp.exp2(s - m)
            l = jnp.sum(p, axis=1, keepdims=True)
            o_ref[part, :] = dot_nn(p.astype(BF16), values)
            m_ref[part, :] = jnp.broadcast_to(m, (BLOCK, HD))
            l_ref[part, :] = jnp.broadcast_to(l, (BLOCK, HD))

    shape = jax.ShapeDtypeStruct((rows, 2 * HD), F32)
    out = pl.BlockSpec((tile, HD), lambda h, i, o: (i, h))
    return pl.pallas_call(
        body,
        out_shape=(shape, shape, shape),
        grid_spec=pltpu.PrefetchScalarGridSpec(
            num_scalar_prefetch=1,
            grid=(2, rows // tile),
            in_specs=[
                pl.BlockSpec((tile, HD), lambda h, i, o: (i, o[h])),
                pl.BlockSpec((rows, HD), lambda h, i, o: (0, o[h])),
                pl.BlockSpec((rows, HD), lambda h, i, o: (0, o[h])),
                pl.BlockSpec((per, 1, rows), lambda h, i, o: (i, 0, 0)),
            ],
            out_specs=(out, out, out),
        ),
        compiler_params=params(),
        cost_estimate=cost(8 * rows * rows * HD, 8 * rows * HD * 8),
    )(order, q, k, v, bias)


def other_half(order, q, kv, bias, o, m, l):
    rows = q.shape[0]
    tile = 256
    per = tile // BLOCK

    def body(order_ref, q_ref, k_ref, v_ref, bias_ref, o_ref, m_ref, l_ref, out_ref):
        keys = k_ref[...]
        values = v_ref[...]
        for n in range(per):
            part = slice(n * BLOCK, (n + 1) * BLOCK)
            s = dot_nt(q_ref[part, :], keys) * SCALE2 + bias_ref[n]
            before = m_ref[part, 0:1]
            m = jnp.maximum(before, jnp.max(s, axis=1, keepdims=True))
            p = jnp.exp2(s - m)
            keep = jnp.exp2(before - m)
            total = l_ref[part, 0:1] * keep + jnp.sum(p, axis=1, keepdims=True)
            mixed = o_ref[part, :] * keep + dot_nn(p.astype(BF16), values)
            out_ref[part, :] = (mixed / total).astype(BF16)

    mid = pl.BlockSpec((tile, HD), lambda h, i, o: (i, h))
    return pl.pallas_call(
        body,
        out_shape=jax.ShapeDtypeStruct((rows, 2 * HD), BF16),
        grid_spec=pltpu.PrefetchScalarGridSpec(
            num_scalar_prefetch=1,
            grid=(2, rows // tile),
            in_specs=[
                pl.BlockSpec((tile, HD), lambda h, i, o: (i, o[h])),
                pl.BlockSpec((rows, HD), lambda h, i, o: (0, h)),
                pl.BlockSpec((rows, HD), lambda h, i, o: (0, 2 + h)),
                pl.BlockSpec((per, 1, rows), lambda h, i, o: (i, 0, 0)),
                mid,
                mid,
                mid,
            ],
            out_specs=mid,
        ),
        compiler_params=params(),
        cost_estimate=cost(8 * rows * rows * HD, 8 * rows * HD * 8),
    )(order, q, kv, kv, bias, o, m, l)


def time_attention(owned, rule, frame_of, key_col, key_row):
    rows = owned.shape[0]
    tile = 256

    def body(all_ref, rule_ref, frame_ref, col_ref, row_ref, out_ref):
        start = pl.multiple_of(pl.program_id(0) * tile, tile)
        q = all_ref[pl.ds(start, tile), 0:HD]
        s = dot_nt(q, all_ref[:, HD : 2 * HD]) * SCALE2
        seen = dot_nn(rule_ref[...], frame_ref[...]) > 0.5
        allowed = jnp.logical_and(seen, col_ref[...] == row_ref[...])
        s = jnp.where(allowed, s, -jnp.inf)
        m = jnp.max(s, axis=1, keepdims=True)
        p = jnp.exp2(s - m)
        l = jnp.sum(p, axis=1, keepdims=True)
        out_ref[...] = (dot_nn(p.astype(BF16), all_ref[:, 2 * HD :]) / l).astype(BF16)

    frames = rule.shape[1]
    return pl.pallas_call(
        body,
        out_shape=jax.ShapeDtypeStruct((rows, HD), BF16),
        grid=(rows // tile,),
        in_specs=[
            pl.BlockSpec((rows, 3 * HD), lambda i: (0, 0)),
            pl.BlockSpec((tile, frames), lambda i: (i, 0)),
            pl.BlockSpec((frames, rows), lambda i: (0, 0)),
            pl.BlockSpec((tile, 1), lambda i: (i, 0)),
            pl.BlockSpec((1, rows), lambda i: (0, 0)),
        ],
        out_specs=pl.BlockSpec((tile, HD), lambda i: (i, 0)),
        compiler_params=params(),
        cost_estimate=cost(4 * rows * rows * HD, 8 * rows * HD),
    )(owned, rule, frame_of, key_col, key_row)


def project_spatial(which, parts, weights):
    rows, width = parts[0].shape
    count, cols, _ = weights.shape
    tile = 256

    def body(which_ref, *refs):
        out_ref = refs[-1]
        w_ref = refs[-2]
        total = None
        for n in range(count):
            term = dot_nt(refs[n][...], w_ref[which_ref[n]])
            total = term if total is None else total + term
        out_ref[...] = total

    return pl.pallas_call(
        body,
        out_shape=jax.ShapeDtypeStruct((rows, cols), F32),
        grid_spec=pltpu.PrefetchScalarGridSpec(
            num_scalar_prefetch=1,
            grid=(rows // tile,),
            in_specs=[pl.BlockSpec((tile, width), lambda i, o: (i, 0))] * count
            + [pl.BlockSpec((count, cols, width), lambda i, o: (0, 0, 0))],
            out_specs=pl.BlockSpec((tile, cols), lambda i, o: (i, 0)),
        ),
        compiler_params=params(),
        cost_estimate=cost(2 * rows * cols * width * count, 6 * rows * cols),
    )(which, *parts, weights)


def project_time(which, side, parts, weights, base, dtype):
    rows, width = parts[0].shape
    count, cols, all_rows = weights.shape
    half = cols // 2
    tile = 256
    last = all_rows // width - 1

    def body(which_ref, side_ref, *refs):
        out_ref = refs[-1]
        base_ref = refs[-2]
        w_ref = refs[-3]
        total = base_ref[...]
        for n in range(count):
            total = total + dot_nt(refs[n][...], w_ref[which_ref[n]])
        out_ref[...] = total.astype(dtype)

    return pl.pallas_call(
        body,
        out_shape=jax.ShapeDtypeStruct((rows, half), dtype),
        grid_spec=pltpu.PrefetchScalarGridSpec(
            num_scalar_prefetch=2,
            grid=(rows // tile,),
            in_specs=[pl.BlockSpec((tile, width), lambda i, o, s: (i, 0))] * count
            + [
                pl.BlockSpec((count, half, width), lambda i, o, s: (0, s[0], last)),
                pl.BlockSpec((tile, half), lambda i, o, s: (i, s[0])),
            ],
            out_specs=pl.BlockSpec((tile, half), lambda i, o, s: (i, 0)),
        ),
        compiler_params=params(),
        cost_estimate=cost(2 * rows * half * width * count, 6 * rows * half),
    )(which, side, *parts, weights, base)


def shards(
    shape_yzx,
    query_states,
    key_states,
    value_states,
    spatial_mask,
    temporal_mask,
    temporal_heads,
    out_weight,
):
    ys, zs, xs, cores = shape_yzx
    _, rows, width = query_states.shape
    heads_here = width // HD
    seq_count = ys * zs
    seq_index = lax.axis_index("seq")
    head_index = lax.axis_index("head")
    frames = spatial_mask.shape[0]
    blocks = spatial_mask.shape[1]
    x_index = head_index // cores
    core = head_index % cores
    q, k, v = query_states[0], key_states[0], value_states[0]

    temp = temporal_heads[0] - head_index * heads_here
    first = jnp.where(temp == 0, 1, 0)
    second = jnp.where(temp == 2, 1, 2)
    order = jnp.stack([first, second, temp]).astype(jnp.int32)

    swap = []
    for y in range(ys):
        for z in range(zs):
            for x in range(xs):
                for c in range(cores):
                    here = (y * zs + z) * xs * cores + x * cores + c
                    there = (x * zs + z) * xs * cores + y * cores + c
                    swap.append((here, there))
    w_own = lax.ppermute(weight_blocks(order, out_weight), ("seq", "head"), swap)
    w_all = lax.all_gather(w_own, "seq", axis=0, tiled=False)
    w_all = w_all.reshape(ys, zs * w_own.shape[0], width)

    kv = pick_columns(order, [(k, 0), (k, 1), (v, 0), (v, 1)], 256)
    kv_other = lax.ppermute(kv, "seq", [(s, s ^ 1) for s in range(seq_count)])

    packed = pick_columns(order, [(q, 2), (k, 2), (v, 2)], 256)
    positions = rows // seq_count
    owned = lax.all_to_all(packed.reshape(seq_count, positions, 3 * HD), "seq", 0, 0, tiled=True)
    owned = owned.reshape(rows, 3 * HD)

    parity = seq_index % 2
    mine = lax.dynamic_slice(
        spatial_mask,
        (seq_index // 2, parity * (blocks // 2), jnp.int32(0)),
        (1, blocks // 2, blocks),
    )[0]
    bias = jnp.where(mine > 0, 0.0, -jnp.inf).astype(F32)
    bias = jnp.where(parity == 0, bias, jnp.roll(bias, blocks // 2, axis=1))
    bias = jnp.repeat(bias, BLOCK, axis=1)[:, None, :]
    o, m, l = own_half(order, q, k, v, bias[:, :, :rows])
    spat = other_half(order, q, kv_other, bias[:, :, rows:], o, m, l)

    spot = np.arange(2)[:, None] * rows + np.arange(positions)[None, :]
    spot = (jnp.asarray(spot.reshape(-1), jnp.int32) + seq_index * positions) // BLOCK
    hot = (spot[:, None] == jnp.arange(blocks, dtype=jnp.int32)[None, :]).astype(BF16)
    rule = jnp.dot(
        hot, (temporal_mask > 0).reshape(blocks, -1).astype(BF16), preferred_element_type=F32
    )
    rule = rule.reshape(2 * positions, frames, frames).transpose(1, 0, 2)
    rule = rule.reshape(rows, frames).astype(BF16)
    index = np.arange(rows)
    frame_of = jnp.asarray(np.arange(frames)[:, None] == index[None, :] // (2 * positions), BF16)
    key = (index % (2 * positions)).astype(np.float32)
    time = time_attention(owned, rule, frame_of, jnp.asarray(key[:, None]), jnp.asarray(key[None]))
    returned = lax.all_to_all(time.reshape(seq_count, positions, HD), "seq", 0, 0, tiled=True)
    returned = returned.reshape(rows, HD)

    def along_x(block):
        got = [block]
        for step in range(1, xs):
            route = [(h, (h + step * cores) % (xs * cores)) for h in range(xs * cores)]
            got.append(lax.ppermute(block, "head", route))
        return got

    which = ((x_index + xs - jnp.arange(xs)) % xs).astype(jnp.int32)
    base = project_spatial(which, along_x(spat), w_all)
    time_parts = along_x(returned)
    mine_side = core.astype(jnp.int32).reshape(1)
    for_twin = project_time(which, 1 - mine_side, time_parts, w_all, base, BF16)
    from_twin = lax.ppermute(for_twin, "head", [(h, h ^ 1) for h in range(xs * cores)])
    own = project_time(which, mine_side, time_parts, w_all, base, F32)
    return (own + from_twin.astype(F32)).astype(BF16)[None]


def solution(mesh):
    in_specs = (
        P(None, "seq", "head"),
        P(None, "seq", "head"),
        P(None, "seq", "head"),
        P(),
        P(),
        P("head"),
        P("head", "seq"),
    )
    out_specs = P(None, "seq", "head")
    return jax.shard_map(
        functools.partial(shards, (4, 8, 4, 2)),
        mesh=mesh,
        in_specs=in_specs,
        out_specs=out_specs,
        check_vma=False,
    )
```

```python
import functools
import math

import jax
import jax.numpy as jnp
import numpy as np
from jax import lax
from jax.experimental import pallas as pl
from jax.experimental.pallas import tpu as pltpu
from jax.sharding import PartitionSpec as P

HD = 128
BLOCK = 128
VMEM = 24 * 1024 * 1024
ALL_VMEM = 60 * 1024 * 1024
BF16 = jnp.bfloat16
F32 = jnp.float32
CFG = {'w': 'zlast2', 'pick': 'kvt', 'order': ['kv', 'packed', 'w', 'own', 'r', 'spat', 'x', 'time', 'r', 'r', 'r'], 'after': {'w': ['kv'], 'own': ['first'], 'time': ['spat'], 'r2': ['time'], 'r3': ['x1', 'x2', 'x3'], 'r4': ['returned']}}
LOG2E = math.log2(math.e)
SCALE2 = LOG2E / math.sqrt(HD)
NT = (((1,), (1,)), ((), ()))


def dot_nt(a, b):
    return lax.dot_general(a, b, NT, preferred_element_type=F32)


def dot_nn(a, b):
    return jnp.dot(a, b, preferred_element_type=F32)


def params():
    return pltpu.CompilerParams(vmem_limit_bytes=VMEM)


def cost(flops, moved):
    return pl.CostEstimate(flops=flops // 1000, bytes_accessed=moved // 1000, transcendentals=0)


def smem():
    return pl.BlockSpec(memory_space=pltpu.SMEM)


def vmem():
    return pl.BlockSpec(memory_space=pltpu.VMEM)


def anywhere():
    return pl.BlockSpec(memory_space=pl.ANY)


def hbm():
    return pl.BlockSpec(memory_space=pltpu.HBM)


def start_all(copies):
    for copy in copies:
        copy.start()


def wait_all(copies):
    for copy in copies:
        copy.wait()


def head_lanes(heads_ref, slot):
    temp = lax.rem(heads_ref[0], 3)
    if slot == 0:
        number = jnp.where(temp == 0, 1, 0)
    elif slot == 1:
        number = jnp.where(temp == 2, 1, 2)
    else:
        number = temp
    return pl.ds(pl.multiple_of(number * HD, HD), HD)


def token(block):
    return block[:16, :HD]


def pick(heads, groups, after=()):
    arrays = []
    for array, _ in [move for group in groups for move in group]:
        if not any(array is a for a in arrays):
            arrays.append(array)
    moves = [
        (next(i for i, a in enumerate(arrays) if a is array), slot, g, n)
        for g, group in enumerate(groups)
        for n, (array, slot) in enumerate(group)
    ]

    def body(heads_ref, *refs):
        outs, sems = refs[-1 - len(groups) : -1], refs[-1]
        copies = [
            pltpu.make_async_copy(
                refs[i].at[:, head_lanes(heads_ref, slot)],
                outs[g].at[:, n * HD : (n + 1) * HD],
                sems.at[k],
            )
            for k, (i, slot, g, n) in enumerate(moves)
        ]
        start_all(copies)
        wait_all(copies)

    return pl.pallas_call(
        body,
        out_shape=tuple(
            jax.ShapeDtypeStruct((group[0][0].shape[0], len(group) * HD), BF16) for group in groups
        ),
        in_specs=[smem()] + [hbm()] * len(arrays) + [anywhere()] * len(after),
        out_specs=(vmem(),) * len(groups),
        scratch_shapes=[pltpu.SemaphoreType.DMA((len(moves),))],
        compiler_params=pltpu.CompilerParams(vmem_limit_bytes=ALL_VMEM),
        cost_estimate=cost(0, 4 * len(moves) * arrays[0].size // 3),
    )(heads, *arrays, *after)


def exp_parts(scores, floor):
    top = floor
    for s in scores:
        part = jnp.max(s, axis=0, keepdims=True)
        top = part if top is None else jnp.maximum(top, part)
    raised = [jnp.exp2(s - top) for s in scores]
    total = None
    for p in raised:
        part = jnp.sum(p, axis=0, keepdims=True)
        total = part if total is None else total + part
    weights = jnp.concatenate([p.astype(BF16) for p in raised], axis=0)
    return top, total, weights


def half_scores(keys, queries, bias_ref, base, tile, t):
    blocks = keys.shape[0] // BLOCK
    out = []
    for n in range(blocks):
        s = dot_nt(keys[n * BLOCK : (n + 1) * BLOCK, :], queries) * SCALE2
        out.append(s + bias_ref[base + n : base + n + 1, t * tile : (t + 1) * tile])
    return out


def own_half(order, q, k, v, bias, after):
    rows = q.shape[0]
    tile = 256

    def body(
        order_ref, q_ref, k_ref, v_ref, bias_ref, *refs
    ):
        o_ref, m_ref, l_ref, q_in, k_in, v_in, sems = refs[-7:]
        copies = [
            [
                pltpu.make_async_copy(
                    src.at[:, head_lanes(order_ref, h)], dst.at[h], sems.at[h, i]
                )
                for i, (src, dst) in enumerate(((q_ref, q_in), (k_ref, k_in), (v_ref, v_in)))
            ]
            for h in range(2)
        ]
        for h in range(2):
            start_all(copies[h])
        for h in range(2):
            wait_all(copies[h])
            keys = k_in[h]
            values = v_in[h].T
            for t in range(rows // tile):
                part = slice(t * tile, (t + 1) * tile)
                scores = half_scores(keys, q_in[h, part, :], bias_ref, 0, tile, t)
                top, total, weights = exp_parts(scores, None)
                o_ref[h, :, part] = dot_nn(values, weights)
                m_ref[h : h + 1, part] = top
                l_ref[h : h + 1, part] = total

    small = jax.ShapeDtypeStruct((2, rows), F32)
    held = pltpu.VMEM((2, rows, HD), BF16)
    return pl.pallas_call(
        body,
        out_shape=(jax.ShapeDtypeStruct((2, HD, rows), F32), small, small),
        in_specs=[smem()] + [hbm()] * 3 + [vmem()] + [anywhere()] * len(after),
        out_specs=(vmem(),) * 3,
        scratch_shapes=[held, held, held, pltpu.SemaphoreType.DMA((2, 3))],
        compiler_params=params(),
        cost_estimate=cost(8 * rows * rows * HD, 8 * rows * HD * 4),
    )(order, q, k, v, bias, *after)


def other_half(order, q, kv, bias, o, m, l, after):
    rows = q.shape[0]
    tile = 256

    def body(
        order_ref, q_ref, kv_ref, bias_ref, o_ref, m_ref, l_ref, *refs
    ):
        out_ref, q_in, k_in, v_in, sems = refs[-5:]
        copies = [
            [
                pltpu.make_async_copy(src, dst.at[h], sems.at[h, i])
                for i, (src, dst) in enumerate(
                    (
                        (q_ref.at[:, head_lanes(order_ref, h)], q_in),
                        (kv_ref.at[:, h * HD : (h + 1) * HD], k_in),
                        (kv_ref.at[:, (2 + h) * HD : (3 + h) * HD], v_in),
                    )
                )
            ]
            for h in range(2)
        ]
        for h in range(2):
            start_all(copies[h])
        for h in range(2):
            wait_all(copies[h])
            keys = k_in[h]
            values = v_in[h].T
            for t in range(rows // tile):
                part = slice(t * tile, (t + 1) * tile)
                scores = half_scores(
                    keys, q_in[h, part, :], bias_ref, rows // BLOCK, tile, t
                )
                before = m_ref[h : h + 1, part]
                top, total, weights = exp_parts(scores, before)
                keep = jnp.exp2(before - top)
                total = total + l_ref[h : h + 1, part] * keep
                mixed = o_ref[h, :, part] * keep + dot_nn(values, weights)
                out_ref[part, h * HD : (h + 1) * HD] = (mixed / total).T.astype(BF16)

    held = pltpu.VMEM((2, rows, HD), BF16)
    return pl.pallas_call(
        body,
        out_shape=jax.ShapeDtypeStruct((rows, 2 * HD), BF16),
        in_specs=[smem(), hbm(), anywhere()] + [vmem()] * 4 + [anywhere()] * len(after),
        out_specs=vmem(),
        scratch_shapes=[held, held, held, pltpu.SemaphoreType.DMA((2, 3))],
        compiler_params=params(),
        cost_estimate=cost(8 * rows * rows * HD, 8 * rows * HD * 4),
    )(order, q, kv, bias, o, m, l, *after)


def time_attention(owned, rule, place, after):
    rows = owned.shape[0]
    tile = 256

    def body(all_ref, rule_ref, place_ref, *refs):
        out_ref = refs[-1]
        values = all_ref[:, 2 * HD :].T
        for t in range(rows // tile):
            part = slice(t * tile, (t + 1) * tile)
            scores = []
            for n in range(rows // BLOCK):
                down = slice(n * BLOCK, (n + 1) * BLOCK)
                s = dot_nt(all_ref[down, HD : 2 * HD], all_ref[part, 0:HD]) * SCALE2
                agree = dot_nn(place_ref[down, :], rule_ref[:, part])
                scores.append(jnp.where(agree > 1.5, s, -jnp.inf))
            _, total, weights = exp_parts(scores, None)
            out_ref[part, :] = (dot_nn(values, weights) / total).T.astype(BF16)

    return pl.pallas_call(
        body,
        out_shape=jax.ShapeDtypeStruct((rows, HD), BF16),
        in_specs=[vmem()] * 3 + [anywhere()] * len(after),
        out_specs=vmem(),
        compiler_params=params(),
        cost_estimate=cost(4 * rows * rows * HD, 8 * rows * HD),
    )(owned, rule, place, *after)


def join(*blocks, after=()):
    rows = [b.shape[0] for b in blocks]
    width = blocks[0].shape[1]

    def body(*refs):
        out_ref = refs[-1]
        start = 0
        for ref, held in zip(refs, rows):
            out_ref[start : start + held, :] = ref[...]
            start += held

    return pl.pallas_call(
        body,
        out_shape=jax.ShapeDtypeStruct((sum(rows), width), BF16),
        in_specs=[vmem()] * len(blocks) + [anywhere()] * len(after),
        out_specs=vmem(),
        compiler_params=params(),
        cost_estimate=cost(0, 4 * sum(rows) * width),
    )(*blocks, *after)


def gate(blocks, after):
    def body(*refs):
        count = len(blocks)
        for n in range(count):
            refs[n - count][...] = refs[n][...]

    return pl.pallas_call(
        body,
        out_shape=tuple(jax.ShapeDtypeStruct(b.shape, b.dtype) for b in blocks),
        in_specs=[vmem()] * len(blocks) + [anywhere()] * len(after),
        out_specs=(vmem(),) * len(blocks),
        compiler_params=params(),
        cost_estimate=cost(0, 4 * sum(b.size for b in blocks)),
    )(*blocks, *after)


def gather_weight(blocks, starts, pieces, after):
    each = 96
    count = pieces[0].shape[0] // each
    width = pieces[0].shape[1]

    def body(block_ref, row_ref, *refs):
        out_ref = refs[-1]
        for n in range(len(pieces)):
            start = pl.multiple_of(row_ref[n] * each, each)
            for j in range(count):
                out_ref[block_ref[j], pl.ds(start, each), :] = refs[n][
                    j * each : (j + 1) * each, :
                ]

    return pl.pallas_call(
        body,
        out_shape=jax.ShapeDtypeStruct((count, len(pieces) * each, width), BF16),
        in_specs=[smem(), smem()] + [vmem()] * len(pieces) + [anywhere()] * len(after),
        out_specs=vmem(),
        compiler_params=params(),
        cost_estimate=cost(0, 4 * count * len(pieces) * each * width),
    )(blocks, starts, *pieces, *after)


def project_spatial(which, side, parts, weights):
    rows, width = parts[0].shape
    count, cols, _ = weights.shape
    half = cols // 2
    tile = 256

    def body(which_ref, side_ref, *refs):
        w_ref, twin_ref, own_ref = refs[-3:]
        for out_ref, place in ((twin_ref, 1 - side_ref[0]), (own_ref, side_ref[0])):
            columns = pl.ds(pl.multiple_of(place * half, half), half)
            for t in range(rows // tile):
                part = slice(t * tile, (t + 1) * tile)
                total = None
                for n in range(count):
                    term = dot_nt(refs[n][part, :], w_ref[which_ref[n], columns, 0:width])
                    total = term if total is None else total + term
                out_ref[part, :] = total

    shape = jax.ShapeDtypeStruct((rows, half), F32)
    return pl.pallas_call(
        body,
        out_shape=(shape, shape),
        in_specs=[smem(), smem()] + [vmem()] * (count + 1),
        out_specs=(vmem(), vmem()),
        compiler_params=params(),
        cost_estimate=cost(2 * rows * cols * width * count, 6 * rows * cols),
    )(which, side, *parts, weights)


def project_time(which, side, parts, weights, base, dtype):
    rows, width = parts[0].shape
    count, cols, all_rows = weights.shape
    half = cols // 2
    tile = 256

    def body(which_ref, side_ref, *refs):
        out_ref = refs[-1]
        w_ref, base_ref = refs[count], refs[count + 1]
        columns = pl.ds(pl.multiple_of(side_ref[0] * half, half), half)
        for t in range(rows // tile):
            part = slice(t * tile, (t + 1) * tile)
            total = base_ref[part, :]
            for n in range(count):
                w = w_ref[which_ref[n], columns, all_rows - width : all_rows]
                total = total + dot_nt(refs[n][part, :], w)
            out_ref[part, :] = total.astype(dtype)

    return pl.pallas_call(
        body,
        out_shape=jax.ShapeDtypeStruct((rows, half), dtype),
        in_specs=[smem(), smem()] + [vmem()] * (count + 2),
        out_specs=vmem(),
        compiler_params=params(),
        cost_estimate=cost(2 * rows * half * width * count, 6 * rows * half),
    )(which, side, *parts, weights, base)


def finish(own, other):
    rows, cols = own.shape
    tile = 256
    count = rows // tile

    def body(own_ref, other_ref, out_ref, held, sems):
        copies = []
        for t in range(count):
            part = slice(t * tile, (t + 1) * tile)
            held[part, :] = (own_ref[part, :] + other_ref[part, :].astype(F32)).astype(BF16)
            copies.append(
                pltpu.make_async_copy(held.at[part, :], out_ref.at[part, :], sems.at[t])
            )
            copies[-1].start()
        wait_all(copies)

    return pl.pallas_call(
        body,
        out_shape=jax.ShapeDtypeStruct((rows, cols), BF16),
        in_specs=[vmem(), vmem()],
        out_specs=hbm(),
        scratch_shapes=[pltpu.VMEM((rows, cols), BF16), pltpu.SemaphoreType.DMA((count,))],
        compiler_params=params(),
        cost_estimate=cost(rows * cols, 8 * rows * cols),
    )(own, other)


def shards(
    shape_yzx,
    query_states,
    key_states,
    value_states,
    spatial_mask,
    temporal_mask,
    temporal_heads,
    out_weight,
):
    ys, zs, xs, cores = shape_yzx
    _, rows, width = query_states.shape
    heads_here = width // HD
    seq_count = ys * zs
    seq_index = lax.axis_index("seq")
    head_index = lax.axis_index("head")
    frames = spatial_mask.shape[0]
    blocks = spatial_mask.shape[1]
    x_index = head_index // cores
    core = head_index % cores
    q, k, v = query_states[0], key_states[0], value_states[0]
    weight = out_weight.T

    W_MODE, T = CFG["w"], CFG
    heads = temporal_heads
    if CFG["pick"] == "all":
        kv, packed, w_own = pick(
            heads,
            [
                [(k, 0), (k, 1), (v, 0), (v, 1)],
                [(q, 2), (k, 2), (v, 2)],
                [(weight, n) for n in range(heads_here)],
            ],
        )
    elif CFG["pick"] == "kvw":
        kv, w_own = pick(
            heads,
            [[(k, 0), (k, 1), (v, 0), (v, 1)], [(weight, n) for n in range(heads_here)]],
        )
    elif CFG["pick"] == "kvt":
        kv, packed = pick(
            heads, [[(k, 0), (k, 1), (v, 0), (v, 1)], [(q, 2), (k, 2), (v, 2)]]
        )
        w_own = None
    elif CFG["pick"] == "timew":
        packed, w_own = pick(
            heads,
            [[(q, 2), (k, 2), (v, 2)], [(weight, n) for n in range(heads_here)]],
        )

    def swap(move):
        route = []
        for y in range(ys):
            for z in range(zs):
                for x in range(xs):
                    for c in range(cores):
                        here = (y * zs + z) * xs * cores + x * cores + c
                        there = (x * zs + move(z)) * xs * cores + y * cores + c
                        route.append((here, there))
        return route

    def along_y(block, step):
        route = [(s, (s + step * zs) % seq_count) for s in range(seq_count)]
        return lax.ppermute(block, "seq", route)

    def along_z(block, step):
        route = [(s, s // zs * zs + (s + step) % zs) for s in range(seq_count)]
        return lax.ppermute(block, "seq", route)

    y_index, z_index = seq_index // zs, seq_index % zs
    got = {}

    def make_w(w_own=w_own):
        if W_MODE == "pair":
            w_two = join(
                lax.ppermute(w_own, ("seq", "head"), swap(lambda z: z)),
                lax.ppermute(w_own, ("seq", "head"), swap(lambda z: z ^ 1)),
                after=toks("w_two"),
            )
            got["w_two"] = w_two
            steps = (0, 2, zs - 2, 4)
            got["z"] = [w_two, *[along_z(w_two, step) for step in steps[1:]]]
            return jnp.stack(
                [((z_index + zs - step) % zs) ^ flip for step in steps for flip in (0, 1)]
            ).astype(jnp.int32)
        if W_MODE == "direct":
            got["z"] = [
                lax.ppermute(w_own, ("seq", "head"), swap(lambda z, n=n: (z + n) % zs))
                for n in range(zs)
            ]
            return jnp.stack([(z_index + zs - n) % zs for n in range(zs)]).astype(jnp.int32)
        if w_own is None:
            (w_own,) = pick(heads, [[(weight, n) for n in range(heads_here)]], toks("w"))
        if W_MODE == "zlast2":
            first = lax.ppermute(w_own, ("seq", "head"), swap(lambda z: z))
            got["first"] = first
            got["w_two"] = join(*[first] + [along_y(first, n) for n in range(1, ys)])
            got["up"], got["down"] = [got["w_two"]], [got["w_two"]]
        if W_MODE == "zlast":
            spread = []
            for step in range(ys):
                route = []
                for y in range(ys):
                    for z in range(zs):
                        for x in range(xs):
                            for c in range(cores):
                                here = (y * zs + z) * xs * cores + x * cores + c
                                to = ((x + step) % ys * zs + z) * xs * cores + y * cores + c
                                route.append((here, to))
                spread.append(lax.ppermute(w_own, ("seq", "head"), route))
            got["w_two"] = join(*spread, after=toks("w_two"))
            got["up"], got["down"] = [got["w_two"]], [got["w_two"]]
        if W_MODE == "ring":
            first = lax.ppermute(w_own, ("seq", "head"), swap(lambda z: z))
            got["w_two"] = first
            got["up"], got["down"] = [first], [first]
            ring_step()

    def ring_step():
        n = len(got["up"])
        up, down = got["up"][-1], got["down"][-1]
        if CFG["after"].get(f"r{n}"):
            if n == 1:
                (up,) = gate([up], toks(f"r{n}"))
                down = up
            else:
                up, down = gate([up, down], toks(f"r{n}"))
        got["up"].append(along_z(up, 1))
        got[f"up{n}"] = got["up"][-1]
        if n < zs // 2:
            got["down"].append(along_z(down, -1))
        else:
            up, down = got["up"], got["down"]
            got["z"] = [up[0], up[1], down[1], *up[2:], *down[2:]]

    def w_order():
        order = [0, 1, zs - 1, *range(2, zs // 2 + 1)] + [zs - n for n in range(2, zs // 2)]
        return jnp.stack([(z_index + zs - n) % zs for n in order]).astype(jnp.int32)

    def make_wz():
        z = got["z"]
        if CFG.get("split"):
            got["w_n"] = join(*z[: CFG["split"]], after=toks("w_n"))
            got["w_z"] = join(*z[CFG["split"] :], after=toks("w_z"))
            got["groups"] = [got["w_n"], got["w_z"]]
        else:
            got["w_z"] = join(*z, after=toks("w_z"))
            got["groups"] = [got["w_z"]]

    def toks(name):
        return [got[n] if n == "kv" else token(got[n]) for n in CFG["after"].get(name, ())]

    def make_kv():
        if CFG["pick"] in ("all", "kvw", "kvt"):
            block = kv
        else:
            (block,) = pick(heads, [[(k, 0), (k, 1), (v, 0), (v, 1)]], toks("kv"))
        got["kv"] = block
        got["kv_other"] = lax.ppermute(block, "seq", [(s, s ^ 1) for s in range(seq_count)])

    positions = rows // seq_count

    def make_time():
        if CFG["pick"] in ("all", "timew", "kvt"):
            block = packed
        else:
            (block,) = pick(heads, [[(q, 2), (k, 2), (v, 2)]], toks("packed"))
        got["packed"] = block
        owned = lax.all_to_all(
            block.reshape(seq_count, positions, 3 * HD), "seq", 0, 0, tiled=True
        )
        got["owned"] = owned.reshape(rows, 3 * HD)

    parity = seq_index % 2
    mine = lax.dynamic_slice(
        spatial_mask,
        (seq_index // 2, parity * (blocks // 2), jnp.int32(0)),
        (1, blocks // 2, blocks),
    )[0]
    bias = jnp.where(mine > 0, 0.0, -jnp.inf).astype(F32)
    bias = jnp.where(parity == 0, bias, jnp.roll(bias, blocks // 2, axis=1))
    bias = jnp.repeat(bias.T, BLOCK, axis=1)

    spot = np.arange(2)[:, None] * rows + np.arange(positions)[None, :]
    spot = (jnp.asarray(spot.reshape(-1), jnp.int32) + seq_index * positions) // BLOCK
    hot = (spot[:, None] == jnp.arange(blocks, dtype=jnp.int32)[None, :]).astype(BF16)
    rule = jnp.dot(
        hot, (temporal_mask > 0).reshape(blocks, -1).astype(BF16), preferred_element_type=F32
    )
    rule = rule.reshape(2 * positions, frames, frames).transpose(2, 1, 0)
    rule = rule.reshape(frames, rows).astype(BF16)
    index = np.arange(rows)
    frame_hot = index[:, None] // (2 * positions) == np.arange(frames)[None, :]
    key_hot = index[:, None] % (2 * positions) == np.arange(2 * positions)[None, :]
    place = jnp.asarray(np.concatenate([frame_hot, key_hot], axis=1), BF16)
    rule = jnp.concatenate([rule, jnp.asarray(key_hot.T, BF16)], axis=0)
    def along_x(block):
        got = [block]
        for step in range(1, xs):
            route = [(h, (h + step * cores) % (xs * cores)) for h in range(xs * cores)]
            got.append(lax.ppermute(block, "head", route))
        return got

    def make_x():
        got["parts"] = along_x(got["spat"])
        got["x1"], got["x2"], got["x3"] = got["parts"][1:]

    def make_own():
        got["o"], got["m"], got["l"] = own_half(heads, q, k, v, bias, toks("own"))
        got["own"] = got["l"]

    def make_spat():
        got["spat"] = other_half(
            heads, q, got["kv_other"], bias, got["o"], got["m"], got["l"], toks("spat")
        )

    def make_att():
        got["time"] = time_attention(got["owned"], rule, place, toks("time"))
        back = lax.all_to_all(
            got["time"].reshape(seq_count, positions, HD), "seq", 0, 0, tiled=True
        )
        got["returned"] = back.reshape(rows, HD)

    steps = dict(
        x=make_x, wz=make_wz, kv=make_kv, packed=make_time, own=make_own, spat=make_spat, time=make_att
    )
    for name in CFG["order"]:
        if name == "w":
            make_w()
        elif name == "r":
            ring_step()
        else:
            steps[name]()
    w_blocks = jnp.stack([(y_index + ys - n) % ys for n in range(ys)]).astype(jnp.int32)
    w_all = gather_weight(w_blocks, w_order(), got["z"], toks("gather"))
    spat, returned = got["spat"], got["returned"]

    which = ((x_index + xs - jnp.arange(xs)) % xs).astype(jnp.int32)
    side = core.astype(jnp.int32).reshape(1)
    base_twin, base_own = project_spatial(which, side, got["parts"], w_all)
    time_parts = along_x(returned)
    for_twin = project_time(which, 1 - side, time_parts, w_all, base_twin, BF16)
    from_twin = lax.ppermute(for_twin, "head", [(h, h ^ 1) for h in range(xs * cores)])
    own = project_time(which, side, time_parts, w_all, base_own, F32)
    return finish(own, from_twin)[None]


def solution(mesh):
    in_specs = (
        P(None, "seq", "head"),
        P(None, "seq", "head"),
        P(None, "seq", "head"),
        P(),
        P(),
        P("head"),
        P("head", "seq"),
    )
    out_specs = P(None, "seq", "head")
    return jax.shard_map(
        functools.partial(shards, (4, 8, 4, 2)),
        mesh=mesh,
        in_specs=in_specs,
        out_specs=out_specs,
        check_vma=False,
    )
```

```python
import functools
import math

import jax
import jax.numpy as jnp
import numpy as np
from jax import lax
from jax.experimental import pallas as pl
from jax.experimental.pallas import tpu as pltpu
from jax.sharding import PartitionSpec as P

HD = 128
BLOCK = 128
VMEM = 24 * 1024 * 1024
ALL_VMEM = 60 * 1024 * 1024
BF16 = jnp.bfloat16
F32 = jnp.float32
CFG = {'w': 'zlast2', 'pick': 'kvt', 'order': ['kv', 'packed', 'w', 'own', 'r', 'spat', 'x', 'time', 'r', 'r', 'r'], 'after': {'w': ['kv'], 'own': ['first'], 'time': ['spat'], 'r2': ['time'], 'r3': ['x1', 'x2', 'x3'], 'r4': ['returned']}, 'tok': ['first', 'spat', 'returned']}
LOG2E = math.log2(math.e)
SCALE2 = LOG2E / math.sqrt(HD)
NT = (((1,), (1,)), ((), ()))


def dot_nt(a, b):
    return lax.dot_general(a, b, NT, preferred_element_type=F32)


def dot_nn(a, b):
    return jnp.dot(a, b, preferred_element_type=F32)


def params():
    return pltpu.CompilerParams(vmem_limit_bytes=VMEM)


def cost(flops, moved):
    return pl.CostEstimate(flops=flops // 1000, bytes_accessed=moved // 1000, transcendentals=0)


def smem():
    return pl.BlockSpec(memory_space=pltpu.SMEM)


def vmem():
    return pl.BlockSpec(memory_space=pltpu.VMEM)


def anywhere():
    return pl.BlockSpec(memory_space=pl.ANY)


def hbm():
    return pl.BlockSpec(memory_space=pltpu.HBM)


def start_all(copies):
    for copy in copies:
        copy.start()


def wait_all(copies):
    for copy in copies:
        copy.wait()


def head_lanes(heads_ref, slot):
    temp = lax.rem(heads_ref[0], 3)
    if slot == 0:
        number = jnp.where(temp == 0, 1, 0)
    elif slot == 1:
        number = jnp.where(temp == 2, 1, 2)
    else:
        number = temp
    return pl.ds(pl.multiple_of(number * HD, HD), HD)


def token(block):
    return block[:16, :HD]


def pick(heads, groups, after=()):
    arrays = []
    for array, _ in [move for group in groups for move in group]:
        if not any(array is a for a in arrays):
            arrays.append(array)
    moves = [
        (next(i for i, a in enumerate(arrays) if a is array), slot, g, n)
        for g, group in enumerate(groups)
        for n, (array, slot) in enumerate(group)
    ]

    def body(heads_ref, *refs):
        outs, sems = refs[-1 - len(groups) : -1], refs[-1]
        copies = [
            pltpu.make_async_copy(
                refs[i].at[:, head_lanes(heads_ref, slot)],
                outs[g].at[:, n * HD : (n + 1) * HD],
                sems.at[k],
            )
            for k, (i, slot, g, n) in enumerate(moves)
        ]
        start_all(copies)
        wait_all(copies)

    return pl.pallas_call(
        body,
        out_shape=tuple(
            jax.ShapeDtypeStruct((group[0][0].shape[0], len(group) * HD), BF16) for group in groups
        ),
        in_specs=[smem()] + [hbm()] * len(arrays) + [anywhere()] * len(after),
        out_specs=(vmem(),) * len(groups),
        scratch_shapes=[pltpu.SemaphoreType.DMA((len(moves),))],
        compiler_params=pltpu.CompilerParams(vmem_limit_bytes=ALL_VMEM),
        cost_estimate=cost(0, 4 * len(moves) * arrays[0].size // 3),
    )(heads, *arrays, *after)


def exp_parts(scores, floor):
    top = floor
    for s in scores:
        part = jnp.max(s, axis=0, keepdims=True)
        top = part if top is None else jnp.maximum(top, part)
    raised = [jnp.exp2(s - top) for s in scores]
    total = None
    for p in raised:
        part = jnp.sum(p, axis=0, keepdims=True)
        total = part if total is None else total + part
    weights = jnp.concatenate([p.astype(BF16) for p in raised], axis=0)
    return top, total, weights


def half_scores(keys, queries, bias_ref, base, tile, t):
    blocks = keys.shape[0] // BLOCK
    out = []
    for n in range(blocks):
        s = dot_nt(keys[n * BLOCK : (n + 1) * BLOCK, :], queries) * SCALE2
        out.append(s + bias_ref[base + n : base + n + 1, t * tile : (t + 1) * tile])
    return out


def own_half(order, q, k, v, bias, after):
    rows = q.shape[0]
    tile = 256

    def body(
        order_ref, q_ref, k_ref, v_ref, bias_ref, *refs
    ):
        o_ref, m_ref, l_ref, q_in, k_in, v_in, sems = refs[-7:]
        copies = [
            [
                pltpu.make_async_copy(
                    src.at[:, head_lanes(order_ref, h)], dst.at[h], sems.at[h, i]
                )
                for i, (src, dst) in enumerate(((q_ref, q_in), (k_ref, k_in), (v_ref, v_in)))
            ]
            for h in range(2)
        ]
        for h in range(2):
            start_all(copies[h])
        for h in range(2):
            wait_all(copies[h])
            keys = k_in[h]
            values = v_in[h].T
            for t in range(rows // tile):
                part = slice(t * tile, (t + 1) * tile)
                scores = half_scores(keys, q_in[h, part, :], bias_ref, 0, tile, t)
                top, total, weights = exp_parts(scores, None)
                o_ref[h, :, part] = dot_nn(values, weights)
                m_ref[h : h + 1, part] = top
                l_ref[h : h + 1, part] = total

    small = jax.ShapeDtypeStruct((2, rows), F32)
    held = pltpu.VMEM((2, rows, HD), BF16)
    return pl.pallas_call(
        body,
        out_shape=(jax.ShapeDtypeStruct((2, HD, rows), F32), small, small),
        in_specs=[smem()] + [hbm()] * 3 + [vmem()] + [anywhere()] * len(after),
        out_specs=(vmem(),) * 3,
        scratch_shapes=[held, held, held, pltpu.SemaphoreType.DMA((2, 3))],
        compiler_params=params(),
        cost_estimate=cost(8 * rows * rows * HD, 8 * rows * HD * 4),
    )(order, q, k, v, bias, *after)


def other_half(order, q, kv, bias, o, m, l, after):
    rows = q.shape[0]
    tile = 256

    def body(
        order_ref, q_ref, kv_ref, bias_ref, o_ref, m_ref, l_ref, *refs
    ):
        out_ref, q_in, k_in, v_in, sems = refs[-5:]
        copies = [
            [
                pltpu.make_async_copy(src, dst.at[h], sems.at[h, i])
                for i, (src, dst) in enumerate(
                    (
                        (q_ref.at[:, head_lanes(order_ref, h)], q_in),
                        (kv_ref.at[:, h * HD : (h + 1) * HD], k_in),
                        (kv_ref.at[:, (2 + h) * HD : (3 + h) * HD], v_in),
                    )
                )
            ]
            for h in range(2)
        ]
        for h in range(2):
            start_all(copies[h])
        for h in range(2):
            wait_all(copies[h])
            keys = k_in[h]
            values = v_in[h].T
            for t in range(rows // tile):
                part = slice(t * tile, (t + 1) * tile)
                scores = half_scores(
                    keys, q_in[h, part, :], bias_ref, rows // BLOCK, tile, t
                )
                before = m_ref[h : h + 1, part]
                top, total, weights = exp_parts(scores, before)
                keep = jnp.exp2(before - top)
                total = total + l_ref[h : h + 1, part] * keep
                mixed = o_ref[h, :, part] * keep + dot_nn(values, weights)
                out_ref[part, h * HD : (h + 1) * HD] = (mixed / total).T.astype(BF16)

    held = pltpu.VMEM((2, rows, HD), BF16)
    return pl.pallas_call(
        body,
        out_shape=jax.ShapeDtypeStruct((rows, 2 * HD), BF16),
        in_specs=[smem(), hbm(), anywhere()] + [vmem()] * 4 + [anywhere()] * len(after),
        out_specs=vmem(),
        scratch_shapes=[held, held, held, pltpu.SemaphoreType.DMA((2, 3))],
        compiler_params=params(),
        cost_estimate=cost(8 * rows * rows * HD, 8 * rows * HD * 4),
    )(order, q, kv, bias, o, m, l, *after)


def time_attention(owned, rule, place, after):
    rows = owned.shape[0]
    tile = 256

    def body(all_ref, rule_ref, place_ref, *refs):
        out_ref = refs[-1]
        values = all_ref[:, 2 * HD :].T
        for t in range(rows // tile):
            part = slice(t * tile, (t + 1) * tile)
            scores = []
            for n in range(rows // BLOCK):
                down = slice(n * BLOCK, (n + 1) * BLOCK)
                s = dot_nt(all_ref[down, HD : 2 * HD], all_ref[part, 0:HD]) * SCALE2
                agree = dot_nn(place_ref[down, :], rule_ref[:, part])
                scores.append(jnp.where(agree > 1.5, s, -jnp.inf))
            _, total, weights = exp_parts(scores, None)
            out_ref[part, :] = (dot_nn(values, weights) / total).T.astype(BF16)

    return pl.pallas_call(
        body,
        out_shape=jax.ShapeDtypeStruct((rows, HD), BF16),
        in_specs=[vmem()] * 3 + [anywhere()] * len(after),
        out_specs=vmem(),
        compiler_params=params(),
        cost_estimate=cost(4 * rows * rows * HD, 8 * rows * HD),
    )(owned, rule, place, *after)


def join(*blocks, after=()):
    rows = [b.shape[0] for b in blocks]
    width = blocks[0].shape[1]

    def body(*refs):
        out_ref = refs[-1]
        start = 0
        for ref, held in zip(refs, rows):
            out_ref[start : start + held, :] = ref[...]
            start += held

    return pl.pallas_call(
        body,
        out_shape=jax.ShapeDtypeStruct((sum(rows), width), BF16),
        in_specs=[vmem()] * len(blocks) + [anywhere()] * len(after),
        out_specs=vmem(),
        compiler_params=params(),
        cost_estimate=cost(0, 4 * sum(rows) * width),
    )(*blocks, *after)


def gate(blocks, after):
    def body(*refs):
        pass

    return pl.pallas_call(
        body,
        out_shape=tuple(jax.ShapeDtypeStruct(b.shape, b.dtype) for b in blocks),
        in_specs=[anywhere()] * (len(blocks) + len(after)),
        out_specs=(anywhere(),) * len(blocks),
        input_output_aliases={n: n for n in range(len(blocks))},
        compiler_params=params(),
        cost_estimate=cost(0, 0),
    )(*blocks, *after)


def gather_weight(blocks, starts, pieces, after):
    each = 96
    count = pieces[0].shape[0] // each
    width = pieces[0].shape[1]

    def body(block_ref, row_ref, *refs):
        out_ref = refs[-1]
        for n in range(len(pieces)):
            start = pl.multiple_of(row_ref[n] * each, each)
            for j in range(count):
                out_ref[block_ref[j], pl.ds(start, each), :] = refs[n][
                    j * each : (j + 1) * each, :
                ]

    return pl.pallas_call(
        body,
        out_shape=jax.ShapeDtypeStruct((count, len(pieces) * each, width), BF16),
        in_specs=[smem(), smem()] + [vmem()] * len(pieces) + [anywhere()] * len(after),
        out_specs=vmem(),
        compiler_params=params(),
        cost_estimate=cost(0, 4 * count * len(pieces) * each * width),
    )(blocks, starts, *pieces, *after)


def project_spatial(which, side, parts, weights):
    rows, width = parts[0].shape
    count, cols, _ = weights.shape
    half = cols // 2
    tile = 256

    def body(which_ref, side_ref, *refs):
        w_ref, twin_ref, own_ref = refs[-3:]
        for out_ref, place in ((twin_ref, 1 - side_ref[0]), (own_ref, side_ref[0])):
            columns = pl.ds(pl.multiple_of(place * half, half), half)
            for t in range(rows // tile):
                part = slice(t * tile, (t + 1) * tile)
                total = None
                for n in range(count):
                    term = dot_nt(refs[n][part, :], w_ref[which_ref[n], columns, 0:width])
                    total = term if total is None else total + term
                out_ref[part, :] = total

    shape = jax.ShapeDtypeStruct((rows, half), F32)
    return pl.pallas_call(
        body,
        out_shape=(shape, shape),
        in_specs=[smem(), smem()] + [vmem()] * (count + 1),
        out_specs=(vmem(), vmem()),
        compiler_params=params(),
        cost_estimate=cost(2 * rows * cols * width * count, 6 * rows * cols),
    )(which, side, *parts, weights)


def project_time(which, side, parts, weights, base, dtype):
    rows, width = parts[0].shape
    count, cols, all_rows = weights.shape
    half = cols // 2
    tile = 256

    def body(which_ref, side_ref, *refs):
        out_ref = refs[-1]
        w_ref, base_ref = refs[count], refs[count + 1]
        columns = pl.ds(pl.multiple_of(side_ref[0] * half, half), half)
        for t in range(rows // tile):
            part = slice(t * tile, (t + 1) * tile)
            total = base_ref[part, :]
            for n in range(count):
                w = w_ref[which_ref[n], columns, all_rows - width : all_rows]
                total = total + dot_nt(refs[n][part, :], w)
            out_ref[part, :] = total.astype(dtype)

    return pl.pallas_call(
        body,
        out_shape=jax.ShapeDtypeStruct((rows, half), dtype),
        in_specs=[smem(), smem()] + [vmem()] * (count + 2),
        out_specs=vmem(),
        compiler_params=params(),
        cost_estimate=cost(2 * rows * half * width * count, 6 * rows * half),
    )(which, side, *parts, weights, base)


def finish(own, other):
    rows, cols = own.shape
    tile = 256
    count = rows // tile

    def body(own_ref, other_ref, out_ref, held, sems):
        copies = []
        for t in range(count):
            part = slice(t * tile, (t + 1) * tile)
            held[part, :] = (own_ref[part, :] + other_ref[part, :].astype(F32)).astype(BF16)
            copies.append(
                pltpu.make_async_copy(held.at[part, :], out_ref.at[part, :], sems.at[t])
            )
            copies[-1].start()
        wait_all(copies)

    return pl.pallas_call(
        body,
        out_shape=jax.ShapeDtypeStruct((rows, cols), BF16),
        in_specs=[vmem(), vmem()],
        out_specs=hbm(),
        scratch_shapes=[pltpu.VMEM((rows, cols), BF16), pltpu.SemaphoreType.DMA((count,))],
        compiler_params=params(),
        cost_estimate=cost(rows * cols, 8 * rows * cols),
    )(own, other)


def shards(
    shape_yzx,
    query_states,
    key_states,
    value_states,
    spatial_mask,
    temporal_mask,
    temporal_heads,
    out_weight,
):
    ys, zs, xs, cores = shape_yzx
    _, rows, width = query_states.shape
    heads_here = width // HD
    seq_count = ys * zs
    seq_index = lax.axis_index("seq")
    head_index = lax.axis_index("head")
    frames = spatial_mask.shape[0]
    blocks = spatial_mask.shape[1]
    x_index = head_index // cores
    core = head_index % cores
    q, k, v = query_states[0], key_states[0], value_states[0]
    weight = out_weight.T

    W_MODE, T = CFG["w"], CFG
    heads = temporal_heads
    if CFG["pick"] == "all":
        kv, packed, w_own = pick(
            heads,
            [
                [(k, 0), (k, 1), (v, 0), (v, 1)],
                [(q, 2), (k, 2), (v, 2)],
                [(weight, n) for n in range(heads_here)],
            ],
        )
    elif CFG["pick"] == "kvw":
        kv, w_own = pick(
            heads,
            [[(k, 0), (k, 1), (v, 0), (v, 1)], [(weight, n) for n in range(heads_here)]],
        )
    elif CFG["pick"] == "kvt":
        kv, packed = pick(
            heads, [[(k, 0), (k, 1), (v, 0), (v, 1)], [(q, 2), (k, 2), (v, 2)]]
        )
        w_own = None
    elif CFG["pick"] == "timew":
        packed, w_own = pick(
            heads,
            [[(q, 2), (k, 2), (v, 2)], [(weight, n) for n in range(heads_here)]],
        )

    def swap(move):
        route = []
        for y in range(ys):
            for z in range(zs):
                for x in range(xs):
                    for c in range(cores):
                        here = (y * zs + z) * xs * cores + x * cores + c
                        there = (x * zs + move(z)) * xs * cores + y * cores + c
                        route.append((here, there))
        return route

    def along_y(block, step):
        route = [(s, (s + step * zs) % seq_count) for s in range(seq_count)]
        return lax.ppermute(block, "seq", route)

    def along_z(block, step):
        route = [(s, s // zs * zs + (s + step) % zs) for s in range(seq_count)]
        return lax.ppermute(block, "seq", route)

    y_index, z_index = seq_index // zs, seq_index % zs
    got = {}

    def make_w(w_own=w_own):
        if W_MODE == "pair":
            w_two = join(
                lax.ppermute(w_own, ("seq", "head"), swap(lambda z: z)),
                lax.ppermute(w_own, ("seq", "head"), swap(lambda z: z ^ 1)),
                after=toks("w_two"),
            )
            got["w_two"] = w_two
            steps = (0, 2, zs - 2, 4)
            got["z"] = [w_two, *[along_z(w_two, step) for step in steps[1:]]]
            return jnp.stack(
                [((z_index + zs - step) % zs) ^ flip for step in steps for flip in (0, 1)]
            ).astype(jnp.int32)
        if W_MODE == "direct":
            got["z"] = [
                lax.ppermute(w_own, ("seq", "head"), swap(lambda z, n=n: (z + n) % zs))
                for n in range(zs)
            ]
            return jnp.stack([(z_index + zs - n) % zs for n in range(zs)]).astype(jnp.int32)
        if w_own is None:
            (w_own,) = pick(heads, [[(weight, n) for n in range(heads_here)]], toks("w"))
        if W_MODE == "zlast2":
            first = lax.ppermute(w_own, ("seq", "head"), swap(lambda z: z))
            got["first"] = first
            got["w_two"] = join(*[first] + [along_y(first, n) for n in range(1, ys)])
            got["up"], got["down"] = [got["w_two"]], [got["w_two"]]
        if W_MODE == "zlast":
            spread = []
            for step in range(ys):
                route = []
                for y in range(ys):
                    for z in range(zs):
                        for x in range(xs):
                            for c in range(cores):
                                here = (y * zs + z) * xs * cores + x * cores + c
                                to = ((x + step) % ys * zs + z) * xs * cores + y * cores + c
                                route.append((here, to))
                spread.append(lax.ppermute(w_own, ("seq", "head"), route))
            got["w_two"] = join(*spread, after=toks("w_two"))
            got["up"], got["down"] = [got["w_two"]], [got["w_two"]]
        if W_MODE == "ring":
            first = lax.ppermute(w_own, ("seq", "head"), swap(lambda z: z))
            got["w_two"] = first
            got["up"], got["down"] = [first], [first]
            ring_step()

    def ring_step():
        n = len(got["up"])
        if CFG["after"].get(f"r{n}"):
            if n == zs // 2:
                (got["up"][-1],) = gate([got["up"][-1]], toks(f"r{n}"))
            else:
                got["up"][-1], got["down"][-1] = gate(
                    [got["up"][-1], got["down"][-1]], toks(f"r{n}")
                )
        got["up"].append(along_z(got["up"][-1], 1))
        got[f"up{n}"] = got["up"][-1]
        if n < zs // 2:
            got["down"].append(along_z(got["down"][-1], -1))
        else:
            up, down = got["up"], got["down"]
            got["z"] = [up[0], up[1], down[1], *up[2:], *down[2:]]

    def w_order():
        order = [0, 1, zs - 1, *range(2, zs // 2 + 1)] + [zs - n for n in range(2, zs // 2)]
        return jnp.stack([(z_index + zs - n) % zs for n in order]).astype(jnp.int32)

    def make_wz():
        z = got["z"]
        if CFG.get("split"):
            got["w_n"] = join(*z[: CFG["split"]], after=toks("w_n"))
            got["w_z"] = join(*z[CFG["split"] :], after=toks("w_z"))
            got["groups"] = [got["w_n"], got["w_z"]]
        else:
            got["w_z"] = join(*z, after=toks("w_z"))
            got["groups"] = [got["w_z"]]

    def toks(name):
        return [token(got[n]) if n in CFG.get("tok", ()) else got[n] for n in CFG["after"].get(name, ())]

    def make_kv():
        if CFG["pick"] in ("all", "kvw", "kvt"):
            block = kv
        else:
            (block,) = pick(heads, [[(k, 0), (k, 1), (v, 0), (v, 1)]], toks("kv"))
        got["kv"] = block
        got["kv_other"] = lax.ppermute(block, "seq", [(s, s ^ 1) for s in range(seq_count)])

    positions = rows // seq_count

    def make_time():
        if CFG["pick"] in ("all", "timew", "kvt"):
            block = packed
        else:
            (block,) = pick(heads, [[(q, 2), (k, 2), (v, 2)]], toks("packed"))
        got["packed"] = block
        owned = lax.all_to_all(
            block.reshape(seq_count, positions, 3 * HD), "seq", 0, 0, tiled=True
        )
        got["owned"] = owned.reshape(rows, 3 * HD)

    parity = seq_index % 2
    mine = lax.dynamic_slice(
        spatial_mask,
        (seq_index // 2, parity * (blocks // 2), jnp.int32(0)),
        (1, blocks // 2, blocks),
    )[0]
    bias = jnp.where(mine > 0, 0.0, -jnp.inf).astype(F32)
    bias = jnp.where(parity == 0, bias, jnp.roll(bias, blocks // 2, axis=1))
    bias = jnp.repeat(bias.T, BLOCK, axis=1)

    spot = np.arange(2)[:, None] * rows + np.arange(positions)[None, :]
    spot = (jnp.asarray(spot.reshape(-1), jnp.int32) + seq_index * positions) // BLOCK
    hot = (spot[:, None] == jnp.arange(blocks, dtype=jnp.int32)[None, :]).astype(BF16)
    rule = jnp.dot(
        hot, (temporal_mask > 0).reshape(blocks, -1).astype(BF16), preferred_element_type=F32
    )
    rule = rule.reshape(2 * positions, frames, frames).transpose(2, 1, 0)
    rule = rule.reshape(frames, rows).astype(BF16)
    index = np.arange(rows)
    frame_hot = index[:, None] // (2 * positions) == np.arange(frames)[None, :]
    key_hot = index[:, None] % (2 * positions) == np.arange(2 * positions)[None, :]
    place = jnp.asarray(np.concatenate([frame_hot, key_hot], axis=1), BF16)
    rule = jnp.concatenate([rule, jnp.asarray(key_hot.T, BF16)], axis=0)
    def along_x(block):
        got = [block]
        for step in range(1, xs):
            route = [(h, (h + step * cores) % (xs * cores)) for h in range(xs * cores)]
            got.append(lax.ppermute(block, "head", route))
        return got

    def make_x():
        got["parts"] = along_x(got["spat"])
        got["x1"], got["x2"], got["x3"] = got["parts"][1:]

    def make_own():
        got["o"], got["m"], got["l"] = own_half(heads, q, k, v, bias, toks("own"))
        got["own"] = got["l"]

    def make_spat():
        got["spat"] = other_half(
            heads, q, got["kv_other"], bias, got["o"], got["m"], got["l"], toks("spat")
        )

    def make_att():
        got["time"] = time_attention(got["owned"], rule, place, toks("time"))
        back = lax.all_to_all(
            got["time"].reshape(seq_count, positions, HD), "seq", 0, 0, tiled=True
        )
        got["returned"] = back.reshape(rows, HD)

    steps = dict(
        x=make_x, wz=make_wz, kv=make_kv, packed=make_time, own=make_own, spat=make_spat, time=make_att
    )
    for name in CFG["order"]:
        if name == "w":
            make_w()
        elif name == "r":
            ring_step()
        else:
            steps[name]()
    w_blocks = jnp.stack([(y_index + ys - n) % ys for n in range(ys)]).astype(jnp.int32)
    w_all = gather_weight(w_blocks, w_order(), got["z"], toks("gather"))
    spat, returned = got["spat"], got["returned"]

    which = ((x_index + xs - jnp.arange(xs)) % xs).astype(jnp.int32)
    side = core.astype(jnp.int32).reshape(1)
    base_twin, base_own = project_spatial(which, side, got["parts"], w_all)
    time_parts = along_x(returned)
    for_twin = project_time(which, 1 - side, time_parts, w_all, base_twin, BF16)
    from_twin = lax.ppermute(for_twin, "head", [(h, h ^ 1) for h in range(xs * cores)])
    own = project_time(which, side, time_parts, w_all, base_own, F32)
    return finish(own, from_twin)[None]


def solution(mesh):
    in_specs = (
        P(None, "seq", "head"),
        P(None, "seq", "head"),
        P(None, "seq", "head"),
        P(),
        P(),
        P("head"),
        P("head", "seq"),
    )
    out_specs = P(None, "seq", "head")
    return jax.shard_map(
        functools.partial(shards, (4, 8, 4, 2)),
        mesh=mesh,
        in_specs=in_specs,
        out_specs=out_specs,
        check_vma=False,
    )
```

```python
import functools
import math

import jax
import jax.numpy as jnp
import numpy as np
from jax import lax
from jax.experimental import pallas as pl
from jax.experimental.pallas import tpu as pltpu
from jax.sharding import PartitionSpec as P

HD = 128
BLOCK = 128
VMEM = 24 * 1024 * 1024
ALL_VMEM = 60 * 1024 * 1024
BF16 = jnp.bfloat16
F32 = jnp.float32
LOG2E = math.log2(math.e)
SCALE2 = LOG2E / math.sqrt(HD)
NT = (((1,), (1,)), ((), ()))


def dot_nt(a, b):
    return lax.dot_general(a, b, NT, preferred_element_type=F32)


def dot_nn(a, b):
    return jnp.dot(a, b, preferred_element_type=F32)


def params():
    return pltpu.CompilerParams(vmem_limit_bytes=VMEM)


def cost(flops, moved):
    return pl.CostEstimate(flops=flops // 1000, bytes_accessed=moved // 1000, transcendentals=0)


def smem():
    return pl.BlockSpec(memory_space=pltpu.SMEM)


def vmem():
    return pl.BlockSpec(memory_space=pltpu.VMEM)


def anywhere():
    return pl.BlockSpec(memory_space=pl.ANY)


def hbm():
    return pl.BlockSpec(memory_space=pltpu.HBM)


def start_all(copies):
    for copy in copies:
        copy.start()


def wait_all(copies):
    for copy in copies:
        copy.wait()


def head_lanes(heads_ref, slot):
    temp = lax.rem(heads_ref[0], 3)
    if slot == 0:
        number = jnp.where(temp == 0, 1, 0)
    elif slot == 1:
        number = jnp.where(temp == 2, 1, 2)
    else:
        number = temp
    return pl.ds(pl.multiple_of(number * HD, HD), HD)


def token(block):
    return block[:16, :HD]


def pick(heads, groups, after=()):
    arrays = []
    for array, _ in [move for group in groups for move in group]:
        if not any(array is a for a in arrays):
            arrays.append(array)
    moves = [
        (next(i for i, a in enumerate(arrays) if a is array), slot, g, n)
        for g, group in enumerate(groups)
        for n, (array, slot) in enumerate(group)
    ]

    def body(heads_ref, *refs):
        outs, sems = refs[-1 - len(groups) : -1], refs[-1]
        copies = [
            pltpu.make_async_copy(
                refs[i].at[:, head_lanes(heads_ref, slot)],
                outs[g].at[:, n * HD : (n + 1) * HD],
                sems.at[k],
            )
            for k, (i, slot, g, n) in enumerate(moves)
        ]
        start_all(copies)
        wait_all(copies)

    return pl.pallas_call(
        body,
        out_shape=tuple(
            jax.ShapeDtypeStruct((group[0][0].shape[0], len(group) * HD), BF16) for group in groups
        ),
        in_specs=[smem()] + [hbm()] * len(arrays) + [anywhere()] * len(after),
        out_specs=(vmem(),) * len(groups),
        scratch_shapes=[pltpu.SemaphoreType.DMA((len(moves),))],
        compiler_params=pltpu.CompilerParams(vmem_limit_bytes=ALL_VMEM),
        cost_estimate=cost(0, 4 * len(moves) * arrays[0].size // 3),
    )(heads, *arrays, *after)


def exp_parts(scores, floor):
    top = floor
    for s in scores:
        part = jnp.max(s, axis=0, keepdims=True)
        top = part if top is None else jnp.maximum(top, part)
    raised = [jnp.exp2(s - top) for s in scores]
    total = None
    for p in raised:
        part = jnp.sum(p, axis=0, keepdims=True)
        total = part if total is None else total + part
    weights = jnp.concatenate([p.astype(BF16) for p in raised], axis=0)
    return top, total, weights


def half_scores(keys, queries, bias_ref, base, tile, t):
    blocks = keys.shape[0] // BLOCK
    out = []
    for n in range(blocks):
        s = dot_nt(keys[n * BLOCK : (n + 1) * BLOCK, :], queries) * SCALE2
        out.append(s + bias_ref[base + n : base + n + 1, t * tile : (t + 1) * tile])
    return out


def own_half(heads, q, k, v, bias, after):
    rows = q.shape[0]
    tile = 256

    def body(
        heads_ref, q_ref, k_ref, v_ref, bias_ref, *refs
    ):
        o_ref, m_ref, l_ref, q_in, k_in, v_in, sems = refs[-7:]
        copies = [
            [
                pltpu.make_async_copy(
                    src.at[:, head_lanes(heads_ref, h)], dst.at[h], sems.at[h, i]
                )
                for i, (src, dst) in enumerate(((q_ref, q_in), (k_ref, k_in), (v_ref, v_in)))
            ]
            for h in range(2)
        ]
        for h in range(2):
            start_all(copies[h])
        for h in range(2):
            wait_all(copies[h])
            keys = k_in[h]
            values = v_in[h].T
            for t in range(rows // tile):
                part = slice(t * tile, (t + 1) * tile)
                scores = half_scores(keys, q_in[h, part, :], bias_ref, 0, tile, t)
                top, total, weights = exp_parts(scores, None)
                o_ref[h, :, part] = dot_nn(values, weights)
                m_ref[h : h + 1, part] = top
                l_ref[h : h + 1, part] = total

    small = jax.ShapeDtypeStruct((2, rows), F32)
    held = pltpu.VMEM((2, rows, HD), BF16)
    return pl.pallas_call(
        body,
        out_shape=(jax.ShapeDtypeStruct((2, HD, rows), F32), small, small),
        in_specs=[smem()] + [hbm()] * 3 + [vmem()] + [anywhere()] * len(after),
        out_specs=(vmem(),) * 3,
        scratch_shapes=[held, held, held, pltpu.SemaphoreType.DMA((2, 3))],
        compiler_params=params(),
        cost_estimate=cost(8 * rows * rows * HD, 8 * rows * HD * 4),
    )(heads, q, k, v, bias, *after)


def other_half(heads, q, kv, bias, o, m, l, after):
    rows = q.shape[0]
    tile = 256

    def body(
        heads_ref, q_ref, kv_ref, bias_ref, o_ref, m_ref, l_ref, *refs
    ):
        out_ref, q_in, k_in, v_in, sems = refs[-5:]
        copies = [
            [
                pltpu.make_async_copy(src, dst.at[h], sems.at[h, i])
                for i, (src, dst) in enumerate(
                    (
                        (q_ref.at[:, head_lanes(heads_ref, h)], q_in),
                        (kv_ref.at[:, h * HD : (h + 1) * HD], k_in),
                        (kv_ref.at[:, (2 + h) * HD : (3 + h) * HD], v_in),
                    )
                )
            ]
            for h in range(2)
        ]
        for h in range(2):
            start_all(copies[h])
        for h in range(2):
            wait_all(copies[h])
            keys = k_in[h]
            values = v_in[h].T
            for t in range(rows // tile):
                part = slice(t * tile, (t + 1) * tile)
                scores = half_scores(
                    keys, q_in[h, part, :], bias_ref, rows // BLOCK, tile, t
                )
                before = m_ref[h : h + 1, part]
                top, total, weights = exp_parts(scores, before)
                keep = jnp.exp2(before - top)
                total = total + l_ref[h : h + 1, part] * keep
                mixed = o_ref[h, :, part] * keep + dot_nn(values, weights)
                out_ref[part, h * HD : (h + 1) * HD] = (mixed / total).T.astype(BF16)

    held = pltpu.VMEM((2, rows, HD), BF16)
    return pl.pallas_call(
        body,
        out_shape=jax.ShapeDtypeStruct((rows, 2 * HD), BF16),
        in_specs=[smem(), hbm(), anywhere()] + [vmem()] * 4 + [anywhere()] * len(after),
        out_specs=vmem(),
        scratch_shapes=[held, held, held, pltpu.SemaphoreType.DMA((2, 3))],
        compiler_params=params(),
        cost_estimate=cost(8 * rows * rows * HD, 8 * rows * HD * 4),
    )(heads, q, kv, bias, o, m, l, *after)


def time_attention(owned, rule, place, after):
    rows = owned.shape[0]
    tile = 256

    def body(all_ref, rule_ref, place_ref, *refs):
        out_ref = refs[-1]
        values = all_ref[:, 2 * HD :].T
        for t in range(rows // tile):
            part = slice(t * tile, (t + 1) * tile)
            scores = []
            for n in range(rows // BLOCK):
                down = slice(n * BLOCK, (n + 1) * BLOCK)
                s = dot_nt(all_ref[down, HD : 2 * HD], all_ref[part, 0:HD]) * SCALE2
                agree = dot_nn(place_ref[down, :], rule_ref[:, part])
                scores.append(jnp.where(agree > 1.5, s, -jnp.inf))
            _, total, weights = exp_parts(scores, None)
            out_ref[part, :] = (dot_nn(values, weights) / total).T.astype(BF16)

    return pl.pallas_call(
        body,
        out_shape=jax.ShapeDtypeStruct((rows, HD), BF16),
        in_specs=[vmem()] * 3 + [anywhere()] * len(after),
        out_specs=vmem(),
        compiler_params=params(),
        cost_estimate=cost(4 * rows * rows * HD, 8 * rows * HD),
    )(owned, rule, place, *after)


def join(*blocks):
    rows = [b.shape[0] for b in blocks]
    width = blocks[0].shape[1]

    def body(*refs):
        out_ref = refs[-1]
        start = 0
        for ref, held in zip(refs, rows):
            out_ref[start : start + held, :] = ref[...]
            start += held

    return pl.pallas_call(
        body,
        out_shape=jax.ShapeDtypeStruct((sum(rows), width), BF16),
        in_specs=[vmem()] * len(blocks),
        out_specs=vmem(),
        compiler_params=params(),
        cost_estimate=cost(0, 4 * sum(rows) * width),
    )(*blocks)


def gate(blocks, after):
    def body(*refs):
        pass

    return pl.pallas_call(
        body,
        out_shape=tuple(jax.ShapeDtypeStruct(b.shape, b.dtype) for b in blocks),
        in_specs=[anywhere()] * (len(blocks) + len(after)),
        out_specs=(anywhere(),) * len(blocks),
        input_output_aliases={n: n for n in range(len(blocks))},
        compiler_params=params(),
        cost_estimate=cost(0, 0),
    )(*blocks, *after)


def gather_weight(blocks, starts, pieces, after):
    each = 96
    count = pieces[0].shape[0] // each
    width = pieces[0].shape[1]

    def body(block_ref, row_ref, *refs):
        out_ref = refs[-1]
        for n in range(len(pieces)):
            start = pl.multiple_of(row_ref[n] * each, each)
            for j in range(count):
                out_ref[block_ref[j], pl.ds(start, each), :] = refs[n][
                    j * each : (j + 1) * each, :
                ]

    return pl.pallas_call(
        body,
        out_shape=jax.ShapeDtypeStruct((count, len(pieces) * each, width), BF16),
        in_specs=[smem(), smem()] + [vmem()] * len(pieces) + [anywhere()] * len(after),
        out_specs=vmem(),
        compiler_params=params(),
        cost_estimate=cost(0, 4 * count * len(pieces) * each * width),
    )(blocks, starts, *pieces, *after)


def project_spatial(which, side, parts, weights):
    rows, width = parts[0].shape
    count, cols, _ = weights.shape
    half = cols // 2
    tile = 256

    def body(which_ref, side_ref, *refs):
        w_ref, twin_ref, own_ref = refs[-3:]
        for out_ref, place in ((twin_ref, 1 - side_ref[0]), (own_ref, side_ref[0])):
            columns = pl.ds(pl.multiple_of(place * half, half), half)
            for t in range(rows // tile):
                part = slice(t * tile, (t + 1) * tile)
                total = None
                for n in range(count):
                    term = dot_nt(refs[n][part, :], w_ref[which_ref[n], columns, 0:width])
                    total = term if total is None else total + term
                out_ref[part, :] = total

    shape = jax.ShapeDtypeStruct((rows, half), F32)
    return pl.pallas_call(
        body,
        out_shape=(shape, shape),
        in_specs=[smem(), smem()] + [vmem()] * (count + 1),
        out_specs=(vmem(), vmem()),
        compiler_params=params(),
        cost_estimate=cost(2 * rows * cols * width * count, 6 * rows * cols),
    )(which, side, *parts, weights)


def project_time(which, side, parts, weights, base, dtype):
    rows, width = parts[0].shape
    count, cols, all_rows = weights.shape
    half = cols // 2
    tile = 256

    def body(which_ref, side_ref, *refs):
        out_ref = refs[-1]
        w_ref, base_ref = refs[count], refs[count + 1]
        columns = pl.ds(pl.multiple_of(side_ref[0] * half, half), half)
        for t in range(rows // tile):
            part = slice(t * tile, (t + 1) * tile)
            total = base_ref[part, :]
            for n in range(count):
                w = w_ref[which_ref[n], columns, all_rows - width : all_rows]
                total = total + dot_nt(refs[n][part, :], w)
            out_ref[part, :] = total.astype(dtype)

    return pl.pallas_call(
        body,
        out_shape=jax.ShapeDtypeStruct((rows, half), dtype),
        in_specs=[smem(), smem()] + [vmem()] * (count + 2),
        out_specs=vmem(),
        compiler_params=params(),
        cost_estimate=cost(2 * rows * half * width * count, 6 * rows * half),
    )(which, side, *parts, weights, base)


def finish(own, other):
    rows, cols = own.shape
    tile = 256
    count = rows // tile

    def body(own_ref, other_ref, out_ref, held, sems):
        copies = []
        for t in range(count):
            part = slice(t * tile, (t + 1) * tile)
            held[part, :] = (own_ref[part, :] + other_ref[part, :].astype(F32)).astype(BF16)
            copies.append(
                pltpu.make_async_copy(held.at[part, :], out_ref.at[part, :], sems.at[t])
            )
            copies[-1].start()
        wait_all(copies)

    return pl.pallas_call(
        body,
        out_shape=jax.ShapeDtypeStruct((rows, cols), BF16),
        in_specs=[vmem(), vmem()],
        out_specs=hbm(),
        scratch_shapes=[pltpu.VMEM((rows, cols), BF16), pltpu.SemaphoreType.DMA((count,))],
        compiler_params=params(),
        cost_estimate=cost(rows * cols, 8 * rows * cols),
    )(own, other)


def shards(
    shape_yzx,
    query_states,
    key_states,
    value_states,
    spatial_mask,
    temporal_mask,
    temporal_heads,
    out_weight,
):
    ys, zs, xs, cores = shape_yzx
    _, rows, width = query_states.shape
    heads_here = width // HD
    seq_count = ys * zs
    seq_index = lax.axis_index("seq")
    head_index = lax.axis_index("head")
    frames = spatial_mask.shape[0]
    blocks = spatial_mask.shape[1]
    x_index = head_index // cores
    core = head_index % cores
    q, k, v = query_states[0], key_states[0], value_states[0]
    weight = out_weight.T

    def along_x(block):
        parts = [block]
        for step in range(1, xs):
            route = [(h, (h + step * cores) % (xs * cores)) for h in range(xs * cores)]
            parts.append(lax.ppermute(block, "head", route))
        return parts

    def along_y(block, step):
        route = [(s, (s + step * zs) % seq_count) for s in range(seq_count)]
        return lax.ppermute(block, "seq", route)

    def along_z(block, step):
        route = [(s, s // zs * zs + (s + step) % zs) for s in range(seq_count)]
        return lax.ppermute(block, "seq", route)

    swap = []
    for y in range(ys):
        for z in range(zs):
            for x in range(xs):
                for c in range(cores):
                    here = (y * zs + z) * xs * cores + x * cores + c
                    there = (x * zs + z) * xs * cores + y * cores + c
                    swap.append((here, there))

    y_index, z_index = seq_index // zs, seq_index % zs
    positions = rows // seq_count
    heads = temporal_heads
    kv, packed = pick(heads, [[(k, 0), (k, 1), (v, 0), (v, 1)], [(q, 2), (k, 2), (v, 2)]])

    parity = seq_index % 2
    mine = lax.dynamic_slice(
        spatial_mask,
        (seq_index // 2, parity * (blocks // 2), jnp.int32(0)),
        (1, blocks // 2, blocks),
    )[0]
    bias = jnp.where(mine > 0, 0.0, -jnp.inf).astype(F32)
    bias = jnp.where(parity == 0, bias, jnp.roll(bias, blocks // 2, axis=1))
    bias = jnp.repeat(bias.T, BLOCK, axis=1)

    spot = np.arange(2)[:, None] * rows + np.arange(positions)[None, :]
    spot = (jnp.asarray(spot.reshape(-1), jnp.int32) + seq_index * positions) // BLOCK
    hot = (spot[:, None] == jnp.arange(blocks, dtype=jnp.int32)[None, :]).astype(BF16)
    rule = jnp.dot(
        hot, (temporal_mask > 0).reshape(blocks, -1).astype(BF16), preferred_element_type=F32
    )
    rule = rule.reshape(2 * positions, frames, frames).transpose(2, 1, 0)
    rule = rule.reshape(frames, rows).astype(BF16)
    index = np.arange(rows)
    frame_hot = index[:, None] // (2 * positions) == np.arange(frames)[None, :]
    key_hot = index[:, None] % (2 * positions) == np.arange(2 * positions)[None, :]
    place = jnp.asarray(np.concatenate([frame_hot, key_hot], axis=1), BF16)
    rule = jnp.concatenate([rule, jnp.asarray(key_hot.T, BF16)], axis=0)

    kv_other = lax.ppermute(kv, "seq", [(s, s ^ 1) for s in range(seq_count)])
    owned = lax.all_to_all(packed.reshape(seq_count, positions, 3 * HD), "seq", 0, 0, tiled=True)
    owned = owned.reshape(rows, 3 * HD)

    (w_own,) = pick(heads, [[(weight, n) for n in range(heads_here)]], [kv])
    first = lax.ppermute(w_own, ("seq", "head"), swap)
    w_y = join(*[first] + [along_y(first, n) for n in range(1, ys)])
    o, m, l = own_half(heads, q, k, v, bias, [token(first)])
    up, down = [w_y, along_z(w_y, 1)], [w_y, along_z(w_y, -1)]

    spat = other_half(heads, q, kv_other, bias, o, m, l, [])
    spat_parts = along_x(spat)
    time = time_attention(owned, rule, place, [token(spat)])
    returned = lax.all_to_all(time.reshape(seq_count, positions, HD), "seq", 0, 0, tiled=True)
    returned = returned.reshape(rows, HD)

    for after in ([time], spat_parts[1:]):
        up[-1], down[-1] = gate([up[-1], down[-1]], after)
        up.append(along_z(up[-1], 1))
        down.append(along_z(down[-1], -1))
    (down[-1],) = gate([down[-1]], [token(returned)])
    down.append(along_z(down[-1], -1))
    pieces = [*up, *down[1:]]
    moved = [*range(zs // 2), *[zs - n for n in range(1, zs // 2 + 1)]]
    starts = jnp.stack([(z_index + zs - n) % zs for n in moved]).astype(jnp.int32)
    w_blocks = jnp.stack([(y_index + ys - n) % ys for n in range(ys)]).astype(jnp.int32)
    w_all = gather_weight(w_blocks, starts, pieces, [])

    which = ((x_index + xs - jnp.arange(xs)) % xs).astype(jnp.int32)
    side = core.astype(jnp.int32).reshape(1)
    base_twin, base_own = project_spatial(which, side, spat_parts, w_all)
    time_parts = along_x(returned)
    for_twin = project_time(which, 1 - side, time_parts, w_all, base_twin, BF16)
    from_twin = lax.ppermute(for_twin, "head", [(h, h ^ 1) for h in range(xs * cores)])
    own = project_time(which, side, time_parts, w_all, base_own, F32)
    return finish(own, from_twin)[None]


def solution(mesh):
    in_specs = (
        P(None, "seq", "head"),
        P(None, "seq", "head"),
        P(None, "seq", "head"),
        P(),
        P(),
        P("head"),
        P("head", "seq"),
    )
    out_specs = P(None, "seq", "head")
    return jax.shard_map(
        functools.partial(shards, (4, 8, 4, 2)),
        mesh=mesh,
        in_specs=in_specs,
        out_specs=out_specs,
        check_vma=False,
    )
```

```python
import functools
import math

import jax
import jax.numpy as jnp
import numpy as np
from jax import lax
from jax.experimental import pallas as pl
from jax.experimental.pallas import tpu as pltpu
from jax.sharding import PartitionSpec as P

HD = 128
BLOCK = 128
VMEM = 24 * 1024 * 1024
ALL_VMEM = 60 * 1024 * 1024
BF16 = jnp.bfloat16
F32 = jnp.float32
LOG2E = math.log2(math.e)
SCALE2 = LOG2E / math.sqrt(HD)
NT = (((1,), (1,)), ((), ()))


def dot_nt(a, b):
    return lax.dot_general(a, b, NT, preferred_element_type=F32)


def dot_nn(a, b):
    return jnp.dot(a, b, preferred_element_type=F32)


def params():
    return pltpu.CompilerParams(vmem_limit_bytes=VMEM)


def cost(flops, moved):
    return pl.CostEstimate(flops=flops // 1000, bytes_accessed=moved // 1000, transcendentals=0)


def smem():
    return pl.BlockSpec(memory_space=pltpu.SMEM)


def vmem():
    return pl.BlockSpec(memory_space=pltpu.VMEM)


def anywhere():
    return pl.BlockSpec(memory_space=pl.ANY)


def hbm():
    return pl.BlockSpec(memory_space=pltpu.HBM)


def start_all(copies):
    for copy in copies:
        copy.start()


def wait_all(copies):
    for copy in copies:
        copy.wait()


def head_lanes(heads_ref, slot):
    temp = lax.rem(heads_ref[0], 3)
    if slot == 0:
        number = jnp.where(temp == 0, 1, 0)
    elif slot == 1:
        number = jnp.where(temp == 2, 1, 2)
    else:
        number = temp
    return pl.ds(pl.multiple_of(number * HD, HD), HD)


def token(block):
    return block[:16, :HD]


def pick(heads, groups, after=()):
    arrays = []
    for array, _ in [move for group in groups for move in group]:
        if not any(array is a for a in arrays):
            arrays.append(array)
    moves = [
        (next(i for i, a in enumerate(arrays) if a is array), slot, g, n)
        for g, group in enumerate(groups)
        for n, (array, slot) in enumerate(group)
    ]

    def body(heads_ref, *refs):
        outs, sems = refs[-1 - len(groups) : -1], refs[-1]
        copies = [
            pltpu.make_async_copy(
                refs[i].at[:, head_lanes(heads_ref, slot)],
                outs[g].at[:, n * HD : (n + 1) * HD],
                sems.at[k],
            )
            for k, (i, slot, g, n) in enumerate(moves)
        ]
        start_all(copies)
        wait_all(copies)

    return pl.pallas_call(
        body,
        out_shape=tuple(
            jax.ShapeDtypeStruct((group[0][0].shape[0], len(group) * HD), BF16) for group in groups
        ),
        in_specs=[smem()] + [hbm()] * len(arrays) + [anywhere()] * len(after),
        out_specs=(vmem(),) * len(groups),
        scratch_shapes=[pltpu.SemaphoreType.DMA((len(moves),))],
        compiler_params=pltpu.CompilerParams(vmem_limit_bytes=ALL_VMEM),
        cost_estimate=cost(0, 4 * len(moves) * arrays[0].size // 3),
    )(heads, *arrays, *after)


def exp_parts(scores, floor):
    top = floor
    for s in scores:
        part = jnp.max(s, axis=0, keepdims=True)
        top = part if top is None else jnp.maximum(top, part)
    raised = [jnp.exp2(s - top) for s in scores]
    total = None
    for p in raised:
        part = jnp.sum(p, axis=0, keepdims=True)
        total = part if total is None else total + part
    weights = jnp.concatenate([p.astype(BF16) for p in raised], axis=0)
    return top, total, weights


def half_scores(keys, queries, bias_ref, base, tile, t):
    blocks = keys.shape[0] // BLOCK
    out = []
    for n in range(blocks):
        s = dot_nt(keys[n * BLOCK : (n + 1) * BLOCK, :], queries) * SCALE2
        out.append(s + bias_ref[base + n : base + n + 1, t * tile : (t + 1) * tile])
    return out


def own_half(heads, q, k, v, bias, after):
    rows = q.shape[0]
    tile = 256

    def body(
        heads_ref, q_ref, k_ref, v_ref, bias_ref, *refs
    ):
        o_ref, m_ref, l_ref, q_in, k_in, v_in, sems = refs[-7:]
        copies = [
            [
                pltpu.make_async_copy(
                    src.at[:, head_lanes(heads_ref, h)], dst.at[h], sems.at[h, i]
                )
                for i, (src, dst) in enumerate(((q_ref, q_in), (k_ref, k_in), (v_ref, v_in)))
            ]
            for h in range(2)
        ]
        for h in range(2):
            start_all(copies[h])
        for h in range(2):
            wait_all(copies[h])
            keys = k_in[h]
            values = v_in[h].T
            for t in range(rows // tile):
                part = slice(t * tile, (t + 1) * tile)
                scores = half_scores(keys, q_in[h, part, :], bias_ref, 0, tile, t)
                top, total, weights = exp_parts(scores, None)
                o_ref[h, :, part] = dot_nn(values, weights)
                m_ref[h : h + 1, part] = top
                l_ref[h : h + 1, part] = total

    small = jax.ShapeDtypeStruct((2, rows), F32)
    held = pltpu.VMEM((2, rows, HD), BF16)
    return pl.pallas_call(
        body,
        out_shape=(jax.ShapeDtypeStruct((2, HD, rows), F32), small, small),
        in_specs=[smem()] + [hbm()] * 3 + [vmem()] + [anywhere()] * len(after),
        out_specs=(vmem(),) * 3,
        scratch_shapes=[held, held, held, pltpu.SemaphoreType.DMA((2, 3))],
        compiler_params=params(),
        cost_estimate=cost(8 * rows * rows * HD, 8 * rows * HD * 4),
    )(heads, q, k, v, bias, *after)


def other_half(heads, q, kv, bias, o, m, l, after):
    rows = q.shape[0]
    tile = 256

    def body(
        heads_ref, q_ref, kv_ref, bias_ref, o_ref, m_ref, l_ref, *refs
    ):
        out_ref, q_in, k_in, v_in, sems = refs[-5:]
        copies = [
            [
                pltpu.make_async_copy(src, dst.at[h], sems.at[h, i])
                for i, (src, dst) in enumerate(
                    (
                        (q_ref.at[:, head_lanes(heads_ref, h)], q_in),
                        (kv_ref.at[:, h * HD : (h + 1) * HD], k_in),
                        (kv_ref.at[:, (2 + h) * HD : (3 + h) * HD], v_in),
                    )
                )
            ]
            for h in range(2)
        ]
        for h in range(2):
            start_all(copies[h])
        for h in range(2):
            wait_all(copies[h])
            keys = k_in[h]
            values = v_in[h].T
            for t in range(rows // tile):
                part = slice(t * tile, (t + 1) * tile)
                scores = half_scores(
                    keys, q_in[h, part, :], bias_ref, rows // BLOCK, tile, t
                )
                before = m_ref[h : h + 1, part]
                top, total, weights = exp_parts(scores, before)
                keep = jnp.exp2(before - top)
                total = total + l_ref[h : h + 1, part] * keep
                mixed = o_ref[h, :, part] * keep + dot_nn(values, weights)
                out_ref[part, h * HD : (h + 1) * HD] = (mixed / total).T.astype(BF16)

    held = pltpu.VMEM((2, rows, HD), BF16)
    return pl.pallas_call(
        body,
        out_shape=jax.ShapeDtypeStruct((rows, 2 * HD), BF16),
        in_specs=[smem(), hbm(), anywhere()] + [vmem()] * 4 + [anywhere()] * len(after),
        out_specs=vmem(),
        scratch_shapes=[held, held, held, pltpu.SemaphoreType.DMA((2, 3))],
        compiler_params=params(),
        cost_estimate=cost(8 * rows * rows * HD, 8 * rows * HD * 4),
    )(heads, q, kv, bias, o, m, l, *after)


def time_attention(owned, rule, place, after):
    rows = owned.shape[0]
    tile = 256

    def body(owned_ref, rule_ref, place_ref, *refs):
        out_ref, all_ref, sems = refs[-3:]
        copies = [
            pltpu.make_async_copy(
                owned_ref.at[:, n * HD : (n + 1) * HD],
                all_ref.at[:, n * HD : (n + 1) * HD],
                sems.at[n],
            )
            for n in range(3)
        ]
        start_all(copies)
        wait_all(copies)
        values = all_ref[:, 2 * HD :].T
        for t in range(rows // tile):
            part = slice(t * tile, (t + 1) * tile)
            scores = []
            for n in range(rows // BLOCK):
                down = slice(n * BLOCK, (n + 1) * BLOCK)
                s = dot_nt(all_ref[down, HD : 2 * HD], all_ref[part, 0:HD]) * SCALE2
                agree = dot_nn(place_ref[down, :], rule_ref[:, part])
                scores.append(jnp.where(agree > 1.5, s, -jnp.inf))
            _, total, weights = exp_parts(scores, None)
            out_ref[part, :] = (dot_nn(values, weights) / total).T.astype(BF16)

    return pl.pallas_call(
        body,
        out_shape=jax.ShapeDtypeStruct((rows, HD), BF16),
        in_specs=[anywhere()] + [vmem()] * 2 + [anywhere()] * len(after),
        out_specs=vmem(),
        scratch_shapes=[pltpu.VMEM((rows, 3 * HD), BF16), pltpu.SemaphoreType.DMA((3,))],
        compiler_params=params(),
        cost_estimate=cost(4 * rows * rows * HD, 8 * rows * HD),
    )(owned, rule, place, *after)


def join(*blocks):
    rows = [b.shape[0] for b in blocks]
    width = blocks[0].shape[1]

    def body(*refs):
        out_ref = refs[-1]
        start = 0
        for ref, held in zip(refs, rows):
            out_ref[start : start + held, :] = ref[...]
            start += held

    return pl.pallas_call(
        body,
        out_shape=jax.ShapeDtypeStruct((sum(rows), width), BF16),
        in_specs=[vmem()] * len(blocks),
        out_specs=vmem(),
        compiler_params=params(),
        cost_estimate=cost(0, 4 * sum(rows) * width),
    )(*blocks)


def gate(blocks, after):
    def body(*refs):
        pass

    return pl.pallas_call(
        body,
        out_shape=tuple(jax.ShapeDtypeStruct(b.shape, b.dtype) for b in blocks),
        in_specs=[anywhere()] * (len(blocks) + len(after)),
        out_specs=(anywhere(),) * len(blocks),
        input_output_aliases={n: n for n in range(len(blocks))},
        compiler_params=params(),
        cost_estimate=cost(0, 0),
    )(*blocks, *after)


def gather_weight(blocks, starts, pieces, after):
    each = 96
    count = pieces[0].shape[0] // each
    width = pieces[0].shape[1]

    def body(block_ref, row_ref, *refs):
        out_ref = refs[-1]
        for n in range(len(pieces)):
            start = pl.multiple_of(row_ref[n] * each, each)
            for j in range(count):
                out_ref[block_ref[j], pl.ds(start, each), :] = refs[n][
                    j * each : (j + 1) * each, :
                ]

    return pl.pallas_call(
        body,
        out_shape=jax.ShapeDtypeStruct((count, len(pieces) * each, width), BF16),
        in_specs=[smem(), smem()] + [vmem()] * len(pieces) + [anywhere()] * len(after),
        out_specs=vmem(),
        compiler_params=params(),
        cost_estimate=cost(0, 4 * count * len(pieces) * each * width),
    )(blocks, starts, *pieces, *after)


def project_spatial(which, side, parts, weights):
    rows, width = parts[0].shape
    count, cols, _ = weights.shape
    half = cols // 2
    tile = 256

    def body(which_ref, side_ref, *refs):
        w_ref, twin_ref, own_ref = refs[-3:]
        for out_ref, place in ((twin_ref, 1 - side_ref[0]), (own_ref, side_ref[0])):
            columns = pl.ds(pl.multiple_of(place * half, half), half)
            for t in range(rows // tile):
                part = slice(t * tile, (t + 1) * tile)
                total = None
                for n in range(count):
                    term = dot_nt(refs[n][part, :], w_ref[which_ref[n], columns, 0:width])
                    total = term if total is None else total + term
                out_ref[part, :] = total

    shape = jax.ShapeDtypeStruct((rows, half), F32)
    return pl.pallas_call(
        body,
        out_shape=(shape, shape),
        in_specs=[smem(), smem()] + [vmem()] * (count + 1),
        out_specs=(vmem(), vmem()),
        compiler_params=params(),
        cost_estimate=cost(2 * rows * cols * width * count, 6 * rows * cols),
    )(which, side, *parts, weights)


def project_time(which, side, parts, weights, base, dtype):
    rows, width = parts[0].shape
    count, cols, all_rows = weights.shape
    half = cols // 2
    tile = 256

    def body(which_ref, side_ref, *refs):
        out_ref = refs[-1]
        w_ref, base_ref = refs[count], refs[count + 1]
        columns = pl.ds(pl.multiple_of(side_ref[0] * half, half), half)
        for t in range(rows // tile):
            part = slice(t * tile, (t + 1) * tile)
            total = base_ref[part, :]
            for n in range(count):
                w = w_ref[which_ref[n], columns, all_rows - width : all_rows]
                total = total + dot_nt(refs[n][part, :], w)
            out_ref[part, :] = total.astype(dtype)

    return pl.pallas_call(
        body,
        out_shape=jax.ShapeDtypeStruct((rows, half), dtype),
        in_specs=[smem(), smem()] + [vmem()] * (count + 2),
        out_specs=vmem(),
        compiler_params=params(),
        cost_estimate=cost(2 * rows * half * width * count, 6 * rows * half),
    )(which, side, *parts, weights, base)


def finish(own, other):
    rows, cols = own.shape
    tile = 256
    count = rows // tile

    def body(own_ref, other_ref, out_ref, held, sems):
        copies = []
        for t in range(count):
            part = slice(t * tile, (t + 1) * tile)
            held[part, :] = (own_ref[part, :] + other_ref[part, :].astype(F32)).astype(BF16)
            copies.append(
                pltpu.make_async_copy(held.at[part, :], out_ref.at[part, :], sems.at[t])
            )
            copies[-1].start()
        wait_all(copies)

    return pl.pallas_call(
        body,
        out_shape=jax.ShapeDtypeStruct((rows, cols), BF16),
        in_specs=[vmem(), vmem()],
        out_specs=hbm(),
        scratch_shapes=[pltpu.VMEM((rows, cols), BF16), pltpu.SemaphoreType.DMA((count,))],
        compiler_params=params(),
        cost_estimate=cost(rows * cols, 8 * rows * cols),
    )(own, other)


def shards(
    shape_yzx,
    query_states,
    key_states,
    value_states,
    spatial_mask,
    temporal_mask,
    temporal_heads,
    out_weight,
):
    ys, zs, xs, cores = shape_yzx
    _, rows, width = query_states.shape
    heads_here = width // HD
    seq_count = ys * zs
    seq_index = lax.axis_index("seq")
    head_index = lax.axis_index("head")
    frames = spatial_mask.shape[0]
    blocks = spatial_mask.shape[1]
    x_index = head_index // cores
    core = head_index % cores
    q, k, v = query_states[0], key_states[0], value_states[0]
    weight = out_weight.T

    def along_x(block):
        parts = [block]
        for step in range(1, xs):
            route = [(h, (h + step * cores) % (xs * cores)) for h in range(xs * cores)]
            parts.append(lax.ppermute(block, "head", route))
        return parts

    def along_y(block, step):
        route = [(s, (s + step * zs) % seq_count) for s in range(seq_count)]
        return lax.ppermute(block, "seq", route)

    def along_z(block, step):
        route = [(s, s // zs * zs + (s + step) % zs) for s in range(seq_count)]
        return lax.ppermute(block, "seq", route)

    swap = []
    for y in range(ys):
        for z in range(zs):
            for x in range(xs):
                for c in range(cores):
                    here = (y * zs + z) * xs * cores + x * cores + c
                    there = (x * zs + z) * xs * cores + y * cores + c
                    swap.append((here, there))

    y_index, z_index = seq_index // zs, seq_index % zs
    positions = rows // seq_count
    heads = temporal_heads
    kv, packed = pick(heads, [[(k, 0), (k, 1), (v, 0), (v, 1)], [(q, 2), (k, 2), (v, 2)]])

    parity = seq_index % 2
    mine = lax.dynamic_slice(
        spatial_mask,
        (seq_index // 2, parity * (blocks // 2), jnp.int32(0)),
        (1, blocks // 2, blocks),
    )[0]
    bias = jnp.where(mine > 0, 0.0, -jnp.inf).astype(F32)
    bias = jnp.where(parity == 0, bias, jnp.roll(bias, blocks // 2, axis=1))
    bias = jnp.repeat(bias.T, BLOCK, axis=1)

    spot = np.arange(2)[:, None] * rows + np.arange(positions)[None, :]
    spot = (jnp.asarray(spot.reshape(-1), jnp.int32) + seq_index * positions) // BLOCK
    hot = (spot[:, None] == jnp.arange(blocks, dtype=jnp.int32)[None, :]).astype(BF16)
    rule = jnp.dot(
        hot, (temporal_mask > 0).reshape(blocks, -1).astype(BF16), preferred_element_type=F32
    )
    rule = rule.reshape(2 * positions, frames, frames).transpose(2, 1, 0)
    rule = rule.reshape(frames, rows).astype(BF16)
    index = np.arange(rows)
    frame_hot = index[:, None] // (2 * positions) == np.arange(frames)[None, :]
    key_hot = index[:, None] % (2 * positions) == np.arange(2 * positions)[None, :]
    place = jnp.asarray(np.concatenate([frame_hot, key_hot], axis=1), BF16)
    rule = jnp.concatenate([rule, jnp.asarray(key_hot.T, BF16)], axis=0)

    kv_other = lax.ppermute(kv, "seq", [(s, s ^ 1) for s in range(seq_count)])
    owned = lax.all_to_all(packed.reshape(seq_count, positions, 3 * HD), "seq", 0, 0, tiled=True)
    owned = owned.reshape(rows, 3 * HD)

    (w_own,) = pick(heads, [[(weight, n) for n in range(heads_here)]], [kv])
    first = lax.ppermute(w_own, ("seq", "head"), swap)
    w_y = join(*[first] + [along_y(first, n) for n in range(1, ys)])
    o, m, l = own_half(heads, q, k, v, bias, [token(first)])
    up, down = [w_y, along_z(w_y, 1)], [w_y, along_z(w_y, -1)]

    spat = other_half(heads, q, kv_other, bias, o, m, l, [])
    spat_parts = along_x(spat)
    time = time_attention(owned, rule, place, [token(spat)])
    returned = lax.all_to_all(time.reshape(seq_count, positions, HD), "seq", 0, 0, tiled=True)
    returned = returned.reshape(rows, HD)

    for after in ([time], spat_parts[1:]):
        up[-1], down[-1] = gate([up[-1], down[-1]], after)
        up.append(along_z(up[-1], 1))
        down.append(along_z(down[-1], -1))
    (down[-1],) = gate([down[-1]], [token(returned)])
    down.append(along_z(down[-1], -1))
    pieces = [*up, *down[1:]]
    moved = [*range(zs // 2), *[zs - n for n in range(1, zs // 2 + 1)]]
    starts = jnp.stack([(z_index + zs - n) % zs for n in moved]).astype(jnp.int32)
    w_blocks = jnp.stack([(y_index + ys - n) % ys for n in range(ys)]).astype(jnp.int32)
    w_all = gather_weight(w_blocks, starts, pieces, [])

    which = ((x_index + xs - jnp.arange(xs)) % xs).astype(jnp.int32)
    side = core.astype(jnp.int32).reshape(1)
    base_twin, base_own = project_spatial(which, side, spat_parts, w_all)
    time_parts = along_x(returned)
    for_twin = project_time(which, 1 - side, time_parts, w_all, base_twin, BF16)
    from_twin = lax.ppermute(for_twin, "head", [(h, h ^ 1) for h in range(xs * cores)])
    own = project_time(which, side, time_parts, w_all, base_own, F32)
    return finish(own, from_twin)[None]


def solution(mesh):
    in_specs = (
        P(None, "seq", "head"),
        P(None, "seq", "head"),
        P(None, "seq", "head"),
        P(),
        P(),
        P("head"),
        P("head", "seq"),
    )
    out_specs = P(None, "seq", "head")
    return jax.shard_map(
        functools.partial(shards, (4, 8, 4, 2)),
        mesh=mesh,
        in_specs=in_specs,
        out_specs=out_specs,
        check_vma=False,
    )
```
